256 devices in a mesh: front: 4 (over x), row: 4 (over y), col: 16 (over z, core).
Axes of the slice: x: 4, y: 4, z: 8, core: 2. Of those that a mesh axis runs over, the one named last changes fastest.
Arguments:
- front: float32 [4, 8, 4, 128, 2, 16, 128], P('front', None, 'row', None, None, 'col')
- child_tiles: float32 [4, 1024, 128, 128], P('front', ('row', 'col')), may hold values from -0.02 to 0.02
- child_owner: int32 [4, 1024, 1], P('front', ('row', 'col')), may hold values from 0 to 15; in each aligned block of 16 rows (0 to 15, 16 to 31, ..., all dimensions but the last counted through in order) at most 2 rows name the same one
- child_row: int32 [4, 1024], P('front', ('row', 'col')), may hold values from 0 to 7
- child_col: int32 [4, 1024], P('front', ('row', 'col')), may hold values from 0 to 1
- front_size: int32 [4], P('front'), may hold values from 1024 to 4096, as said below
Outputs:
- factored: float32 [4, 8, 4, 128, 2, 16, 128], P('front', None, 'row', None, None, 'col')
The draws below stay inside these ranges and needn't reach their ends.
Inputs may be any that keep to these rules, and one draw needn't show every extreme that they name: `child_owner`: among the 16 tiles of one device no value appears more than 2 times. `front_size`: rows and columns of a front beyond its true order are padding.
All inputs are finite; a program needn't handle non-finite values.
Results may differ from the reference program's by a relative error of at most 0.0001.
Values sent between devices are 32-bit elements; how exact they have to be, the bound alone decides.
No kernel may reach another device: no remote copies, remote signals or barrier semaphores. Data moves between devices by JAX's collectives and lax.ppermute only.
A program may use at most 128 MiB of HBM per device.

```python
import math
import jax
import jax.numpy as jnp
import numpy as np
from jax import lax

TILE = 128
ORDER = 4096
PANEL = 1024
CHILD_DEV = 16
CAPACITY = 2
FRONTS = 4
N_ROW = 4
N_COL = 16


def smooth_rows(basis):
    running = basis
    for offset in range(1, 4):
        running = running + jnp.roll(basis, offset, axis=1)
    return 0.5 * running


def draw_front(key, part):
    key = jax.random.fold_in(key, 11)
    basis_key, diag_key = jax.random.split(key, 2)
    basis = smooth_rows(jax.random.uniform(basis_key, (FRONTS, ORDER, ORDER), jnp.float32, -1.0, 1.0))
    gram = jnp.einsum('gik,gjk->gij', basis, basis, precision=lax.Precision.HIGHEST) * (6.0 / ORDER)
    gram = 0.5 * (gram + jnp.swapaxes(gram, 1, 2))
    diagonal = jax.random.uniform(diag_key, (FRONTS, ORDER), jnp.float32, 0.5, 1.0)
    unit = jnp.eye(ORDER, dtype=jnp.float32)
    whole = gram + diagonal[:, :, None] * unit
    return whole.reshape(FRONTS, ORDER // (TILE * N_ROW), N_ROW, TILE, ORDER // (TILE * N_COL), N_COL, TILE)


def draw_child_tiles(key, part):
    key = jax.random.fold_in(key, 31)
    tile_shape = (FRONTS, N_ROW * N_COL * CHILD_DEV, TILE, TILE)
    values = jax.random.uniform(key, tile_shape, jnp.float32, -0.02, 0.02)
    return values


def draw_front_size(key, part):
    key = jax.random.fold_in(key, 23)
    size_key, full_key = jax.random.split(key)
    sizes = jax.random.randint(size_key, (FRONTS,), PANEL, ORDER + 1)
    full_one = jax.random.randint(full_key, (), 0, FRONTS)
    return jnp.where(jnp.arange(FRONTS) == full_one, ORDER, sizes).astype(jnp.int32)


def set_ends(result, own_key, least, high):
    index_at = [jax.random.randint(jax.random.fold_in(own_key, axis), (), 0, length) for axis, length in enumerate(result.shape)]
    longest = result.shape.index(max(result.shape))
    neighbour = index_at[:longest] + [(index_at[longest] + 1) % result.shape[longest]] + index_at[longest + 1:]
    return result.at[tuple(index_at)].set(least).at[tuple(neighbour)].set(high)


def deal_out(rng, own, number, rows, count, top, reach, slope):
    order = jax.random.permutation(rng, count)
    crowded, usual = shares(count, rows * top, reach, slope, True), shares(count, rows * top, reach, slope, False)
    places = jnp.arange(count)

    def named(sizes, offset_by):
        used = int((sizes > 0).sum())
        fixed = max(1, used // 4)
        shifted = fixed + (places - fixed + offset_by * (used - fixed)) % max(1, count - fixed)
        return jnp.zeros((count,), jnp.int32).at[order[jnp.where(places < fixed, places, shifted)]].set(jnp.asarray(sizes, jnp.int32))

    sizes = jnp.where(number % 4 == 0, named(crowded, number // 4), named(usual, number - number // 4 - 1))
    mixed = jax.random.permutation(jax.random.fold_in(own, 3), count)
    giver, sink = mixed[0:count // 2 * 2:2], mixed[1:count // 2 * 2:2]
    slack = jnp.minimum(sizes[giver] - 1, reach - sizes[sink]) // 2
    slack = jnp.where((giver == order[0]) | (sink == order[0]) | (sizes[sink] == 0), 0, jnp.maximum(slack, 0))
    shifted = jax.random.randint(jax.random.fold_in(own, 4), (count // 2,), 0, 1 << 20) % (slack + 1)
    sizes = sizes.at[giver].add(-shifted).at[sink].add(shifted)
    members = jnp.searchsorted(jnp.cumsum(sizes), jnp.arange(rows * top), side="right").astype(jnp.int32)
    listing = members.reshape(top, rows).T
    listing = listing[jax.random.permutation(jax.random.fold_in(own, 1), rows)]
    offset_by = jax.random.randint(jax.random.fold_in(own, 2), (rows, 1), 0, top)
    return jnp.take_along_axis(listing, (jnp.arange(top)[None, :] + offset_by) % top, axis=1)


def shares(amount, total, bound, lean, full):
    weights = [(1 << 20) // math.isqrt(rank ** lean) + 1 for rank in range(1, amount + 1)]
    largest = bound if full else min(bound, max(-(-total // amount), total * weights[0] // sum(weights)))
    least = 1 if total - largest >= amount - 1 else 0
    holding, rest = [largest] + [least] * (amount - 1), total - largest - least * (amount - 1)
    while rest > 0:
        movable = [i for i in range(1, amount) if holding[i] < largest] or [i for i in range(1, amount) if holding[i] < bound]
        mass, remaining = sum([weights[i] for i in movable]), rest
        for i in movable:
            more = min(bound - holding[i], max(1, remaining * weights[i] // mass), rest)
            holding[i] = holding[i] + more
            rest = rest - more
    return np.array(holding)


def setup_inputs(seed: int = 0) -> dict:
    streams_of = jax.random.split(jax.random.key(seed), 7)
    front = draw_front(jax.random.fold_in(streams_of[6], 71), 0)
    child_tiles = draw_child_tiles(jax.random.fold_in(streams_of[6], 71), 0)
    child_owner_keys = jax.random.split(jax.random.fold_in(streams_of[2], 1), FRONTS * (N_ROW * N_COL * CHILD_DEV) // CHILD_DEV)
    child_owner_turns = jax.random.permutation(jax.random.fold_in(streams_of[2], 3), FRONTS * (N_ROW * N_COL * CHILD_DEV) // CHILD_DEV)
    child_owner = jax.vmap(lambda own, number: deal_out(jax.random.fold_in(streams_of[2], 2), own, number, CHILD_DEV, N_COL, 1, CAPACITY, 2))(child_owner_keys, child_owner_turns).reshape((FRONTS, N_ROW * N_COL * CHILD_DEV, 1))
    child_row = set_ends(jax.random.randint(streams_of[3], (FRONTS, N_ROW * N_COL * CHILD_DEV), 0, ORDER // (TILE * N_ROW)), jax.random.fold_in(streams_of[3], 1), 0, (ORDER // (TILE * N_ROW)) - 1).astype(jnp.int32)
    child_col = set_ends(jax.random.randint(streams_of[4], (FRONTS, N_ROW * N_COL * CHILD_DEV), 0, ORDER // (TILE * N_COL)), jax.random.fold_in(streams_of[4], 1), 0, (ORDER // (TILE * N_COL)) - 1).astype(jnp.int32)
    front_size = draw_front_size(jax.random.fold_in(streams_of[6], 71), 0)
    return {"front": front, "child_tiles": child_tiles, "child_owner": child_owner, "child_row": child_row, "child_col": child_col, "front_size": front_size}


HIGH = lax.Precision.HIGHEST

def reference(front, child_tiles, child_owner, child_row, child_col, front_size):
    front_count = front.shape[0]
    tiles_side = ORDER // TILE
    grid = front.reshape(front_count, tiles_side, TILE, tiles_side, TILE).transpose(0, 1, 3, 2, 4)
    holder_row = (jnp.arange(child_tiles.shape[1]) // (N_COL * CHILD_DEV)).astype(jnp.int32)
    for source in range(front_count):
        target = (source + 1) % front_count
        rows_at = child_row[source] * N_ROW + holder_row
        cols_at = child_col[source] * N_COL + child_owner[source, :, 0]
        grid = grid.at[target, rows_at, cols_at].add(child_tiles[source])
    assembled = grid.transpose(0, 1, 3, 2, 4).reshape(front_count, ORDER, ORDER)
    positions = jnp.arange(ORDER)
    results = []
    for which in range(front_count):
        limit = front_size[which]
        inside = (positions[:, None] < limit) & (positions[None, :] < limit)
        padded = jnp.where(inside, assembled[which], jnp.eye(ORDER, dtype=jnp.float32))
        corner = padded[:PANEL, :PANEL]
        factor = jnp.linalg.cholesky(jnp.tril(corner) + jnp.tril(corner, -1).T)
        lower_rows = jax.scipy.linalg.solve_triangular(factor, padded[PANEL:, :PANEL].T, lower=True).T
        schur = padded[PANEL:, PANEL:] - jnp.dot(lower_rows, lower_rows.T, precision=HIGH)
        left_part = jnp.concatenate([factor, lower_rows], 0)
        right_part = jnp.concatenate([jnp.zeros((PANEL, ORDER - PANEL), jnp.float32), schur], 0)
        results.append(jnp.concatenate([left_part, right_part], 1))
    return jnp.stack(results).reshape(front.shape)
```

```python
import jax
import jax.numpy as jnp
from jax import lax
from jax.experimental import pallas as pl
from jax.experimental.pallas import tpu as pltpu
from jax.sharding import PartitionSpec as P

T = 128
G = 8
NB = 8
ROWS = 4
COLS = 16
HIGH = lax.Precision.HIGHEST
VMEM_LIMIT = 48 * 1024 * 1024


def params():
    return pltpu.CompilerParams(vmem_limit_bytes=VMEM_LIMIT)


def dotx(a, b, dims):
    return lax.dot_general(
        a, b, (dims, ((), ())), precision=HIGH, preferred_element_type=jnp.float32
    )


def factor_tile(s_ref, w_ref):
    rows = lax.broadcasted_iota(jnp.int32, (T, T), 0)
    lanes = lax.broadcasted_iota(jnp.int32, (T, T), 1)
    w_ref[...] = (rows == lanes).astype(jnp.float32)
    sub = lax.broadcasted_iota(jnp.int32, (G, T), 0)
    lane = lax.broadcasted_iota(jnp.int32, (G, T), 1)
    count = T // G
    for p in range(count):
        r0 = p * G
        R = s_ref[r0:r0 + G, :]
        W = w_ref[r0:r0 + G, :]
        last = p == count - 1
        splat = [jnp.broadcast_to(R[:, r0 + t:r0 + t + 1], (G, T)) for t in range(G)]
        e = [[None] * G for _ in range(G)]
        for t in range(G):
            for s in range(t + 1):
                e[s][t] = jnp.broadcast_to(splat[t][s:s + 1, :], (G, T))
        a = [jnp.broadcast_to(R[t:t + 1, :], (G, T)) for t in range(G)]
        w = [jnp.broadcast_to(W[t:t + 1, :], (G, T)) for t in range(G)]
        if not last:
            N = s_ref[r0 + G:r0 + 2 * G, :]
            V = w_ref[r0 + G:r0 + 2 * G, :]
            c = [jnp.broadcast_to(N[:, r0 + t:r0 + t + 1], (G, T)) for t in range(G)]
        U = jnp.zeros((G, T), jnp.float32)
        X = jnp.zeros((G, T), jnp.float32)
        for t in range(G):
            rec = 1.0 / e[t][t]
            root = lax.rsqrt(e[t][t])
            m = {}
            for s in range(t + 1, G):
                m[s] = e[t][s] * rec
                for q in range(s, G):
                    e[s][q] = e[s][q] - (e[t][s] * e[t][q]) * rec
            for s in range(t + 1, G):
                a[s] = a[s] - m[s] * a[t]
                w[s] = w[s] - m[s] * w[t]
            U = jnp.where(sub == t, a[t] * root, U)
            X = jnp.where(sub == t, w[t] * root, X)
            if not last:
                for s in range(t + 1, G):
                    c[s] = c[s] - m[s] * c[t]
                ct = c[t] * rec
                N = N - ct * a[t]
                V = V - ct * w[t]
        U = jnp.where(lane >= r0 + sub, U, 0.0)
        s_ref[r0:r0 + G, :] = U
        w_ref[r0:r0 + G, :] = X
        if not last:
            s_ref[r0 + G:r0 + 2 * G, :] = N
            w_ref[r0 + G:r0 + 2 * G, :] = V
        if r0 + 2 * G < T:
            both = jnp.concatenate([U, X], 1)
            prod = dotx(U, both, ((0,), (0,)))
            s_ref[r0 + 2 * G:, :] = s_ref[r0 + 2 * G:, :] - prod[r0 + 2 * G:, :T]
            w_ref[r0 + 2 * G:, :] = w_ref[r0 + 2 * G:, :] - prod[r0 + 2 * G:, T:]


def corner_kernel(ids_ref, own_ref, other_ref, l_ref, w_ref, s_ref):
    z = ids_ref[0]
    h = ids_ref[1]
    r = ids_ref[2]
    rows = lax.broadcasted_iota(jnp.int32, (T, T), 0)
    lanes = lax.broadcasted_iota(jnp.int32, (T, T), 1)
    for s in range(NB):
        j = (z + NB - s) % NB
        for t in range(ROWS):
            i = (r + ROWS - t) % ROWS
            at = pl.multiple_of((i + ROWS * h) * T, T)
            l_ref[j, pl.ds(at, T), :] = own_ref[s, t]
            at = pl.multiple_of((i + ROWS * (1 - h)) * T, T)
            l_ref[j, pl.ds(at, T), :] = other_ref[s, t]
    for j in range(NB):
        d = l_ref[j, j * T:(j + 1) * T, :]
        low = jnp.where(rows >= lanes, d, 0.0)
        strict = jnp.where(rows > lanes, d, 0.0)
        l_ref[j, j * T:(j + 1) * T, :] = low + strict.T
        if j:
            l_ref[j, :j * T, :] = jnp.zeros((j * T, T), jnp.float32)
    for k in range(NB):
        s_ref[...] = l_ref[k, k * T:(k + 1) * T, :]
        factor_tile(s_ref, w_ref.at[k])
        l_ref[k, k * T:(k + 1) * T, :] = s_ref[...].T
        if k < NB - 1:
            X = dotx(l_ref[k, (k + 1) * T:, :], w_ref[k], ((1,), (1,)))
            l_ref[k, (k + 1) * T:, :] = X
            for j in range(k + 1, NB):
                lo = (j - k - 1) * T
                l_ref[j, j * T:, :] = l_ref[j, j * T:, :] - dotx(X[lo:], X[lo:lo + T], ((1,), (1,)))


def body_kernel(l_ref, w_ref, own_ref, right_ref, x_ref, s_ref):
    for k in range(NB):
        x_ref[k, :6 * T, :] = own_ref[k].reshape(6 * T, T)
        x_ref[k, 6 * T:, :] = right_ref[k].reshape(2 * T, T)
    for k in range(NB):
        X = dotx(x_ref[k], w_ref[k], ((1,), (1,)))
        x_ref[k] = X
        for j in range(k + 1, NB):
            x_ref[j] = x_ref[j] - dotx(X, l_ref[k, j * T:(j + 1) * T, :], ((1,), (1,)))
        prod = dotx(X[:768], X[768:], ((1,), (1,)))
        if k == 0:
            s_ref[...] = prod
        else:
            s_ref[...] = s_ref[...] + prod


def scatter_kernel(ids_ref, owner_ref, row_ref, col_ref, tiles_ref, dense_ref, send_ref, count_ref):
    z = ids_ref[0]
    h = ids_ref[1]
    dense_ref[...] = jnp.zeros(dense_ref.shape, jnp.float32)
    for slot in range(2 * COLS):
        send_ref[slot, T:, :] = jnp.zeros((8, T), jnp.float32)
    for o in range(COLS):
        count_ref[o] = 0

    def step(i, carry):
        o = owner_ref[i]
        a = row_ref[i]
        b = col_ref[i]
        corner = jnp.logical_and(jnp.logical_and(b == 0, o < NB), a < 2)

        @pl.when(corner)
        def _():
            p = jnp.bitwise_xor(o, z)
            p = (p & 1) * 4 + (p & 2) + (p // 4)
            q = jnp.bitwise_xor(a, h)
            dense_ref[q, p] = dense_ref[q, p] + tiles_ref[i]

        @pl.when(jnp.logical_not(corner))
        def _():
            slot = 2 * o + count_ref[o]
            count_ref[o] = count_ref[o] + 1
            send_ref[slot, :T, :] = tiles_ref[i]
            mark = (b * 8 + a + 1).astype(jnp.float32)
            send_ref[slot, T:, :] = jnp.full((8, T), mark, jnp.float32)

        return carry

    lax.fori_loop(0, owner_ref.shape[0], step, 0)


def scatter_call(ids, owner, row, col, tiles):
    smem = pl.BlockSpec(memory_space=pltpu.SMEM)
    vmem = pl.BlockSpec(memory_space=pltpu.VMEM)
    return pl.pallas_call(
        scatter_kernel,
        in_specs=[smem, smem, smem, smem, vmem],
        out_specs=[vmem, vmem],
        out_shape=[
            jax.ShapeDtypeStruct((2, NB, T, T), jnp.float32),
            jax.ShapeDtypeStruct((2 * COLS, T + 8, T), jnp.float32),
        ],
        scratch_shapes=[pltpu.SMEM((COLS,), jnp.int32)],
        compiler_params=params(),
    )(ids, owner, row, col, tiles)


def combine_kernel(mark_ref, tiles_ref, out_ref):
    out_ref[...] = jnp.zeros(out_ref.shape, jnp.float32)

    def step(s, carry):
        mark = mark_ref[s] - 1
        a = mark % 8
        b = mark // 8

        @pl.when(jnp.logical_and(mark >= 0, a >= 2))
        def _():
            out_ref[b, a - 2] = out_ref[b, a - 2] + tiles_ref[s, :T, :]

        return carry

    lax.fori_loop(0, 2 * COLS, step, 0)


def combine_call(marks, tiles):
    smem = pl.BlockSpec(memory_space=pltpu.SMEM)
    vmem = pl.BlockSpec(memory_space=pltpu.VMEM)
    return pl.pallas_call(
        combine_kernel,
        in_specs=[smem, vmem],
        out_specs=vmem,
        out_shape=jax.ShapeDtypeStruct((2, 6, T, T), jnp.float32),
        compiler_params=params(),
    )(marks, tiles)


def corner_call(ids, own, other):
    smem = pl.BlockSpec(memory_space=pltpu.SMEM)
    vmem = pl.BlockSpec(memory_space=pltpu.VMEM)
    return pl.pallas_call(
        corner_kernel,
        in_specs=[smem, vmem, vmem],
        out_specs=[vmem, vmem],
        out_shape=[
            jax.ShapeDtypeStruct((NB, NB * T, T), jnp.float32),
            jax.ShapeDtypeStruct((NB, T, T), jnp.float32),
        ],
        scratch_shapes=[pltpu.VMEM((T, T), jnp.float32)],
        compiler_params=params(),
    )(ids, own, other)


def body_call(l, w, own, right):
    vmem = pl.BlockSpec(memory_space=pltpu.VMEM)
    return pl.pallas_call(
        body_kernel,
        in_specs=[vmem] * 4,
        out_specs=[vmem, vmem],
        out_shape=[
            jax.ShapeDtypeStruct((NB, NB * T, T), jnp.float32),
            jax.ShapeDtypeStruct((6 * T, 2 * T), jnp.float32),
        ],
        compiler_params=params(),
    )(l, w, own, right)


def moved(value, axes, pairs):
    return lax.ppermute(value, axes, pairs)


def col_xor(bits):
    return [(i, i ^ bits) for i in range(COLS)]


def on_device(front, child_tiles, child_owner, child_row, child_col, front_size):
    r = lax.axis_index("row")
    c = lax.axis_index("col")
    z = c // 2
    h = c % 2
    limit = front_size[0]
    stored = front.reshape(8, T, 2, T).transpose(2, 0, 1, 3)
    ids = jnp.stack([z, h, r, c]).astype(jnp.int32)

    even = moved(stored[0, 0], "col", [(i, 2 * i) for i in range(NB)])
    odd = moved(stored[0, 1], "col", [(i, 2 * i + 1) for i in range(NB)])
    mine = jnp.where(h == 0, even, odd)

    dense, send = scatter_call(ids, child_owner[0, :, 0], child_row[0], child_col[0], child_tiles[0])
    arrived = lax.all_to_all(send, "col", split_axis=0, concat_axis=0, tiled=True)

    part = dense[0] + moved(dense[1], "col", col_xor(1))
    part = part[:4] + moved(part[4:], "col", col_xor(2))
    part = part[:2] + moved(part[2:], "col", col_xor(4))
    hop = [(f * COLS + i, (f + 1) % 4 * COLS + i) for f in range(4) for i in range(COLS)]
    hop_far = [(s, d // COLS * COLS + (d % COLS ^ 8)) for s, d in hop]
    added = moved(part[0], ("front", "col"), hop) + moved(part[1], ("front", "col"), hop_far)

    rows = jnp.arange(T)[:, None]
    lanes = jnp.arange(T)[None, :]

    def masked(value, tile_row, tile_col):
        i = tile_row * T + rows
        j = tile_col * T + lanes
        return jnp.where((i < limit) & (j < limit), value, (i == j).astype(jnp.float32))

    corner = (mine + added)[None]
    quad = jnp.concatenate(
        [corner] + [moved(corner, "row", [(i, (i + s) % ROWS) for i in range(ROWS)]) for s in (1, 2, 3)], 0
    )
    pieces = [None] * NB
    pieces[0] = quad
    ahead = behind = quad
    for s in range(1, 5):
        ahead = moved(ahead, "col", [(i, (i + 2) % COLS) for i in range(COLS)])
        pieces[s] = ahead
        if s < 4:
            behind = moved(behind, "col", [(i, (i - 2) % COLS) for i in range(COLS)])
            pieces[NB - s] = behind
    own = jnp.stack(pieces)
    other = moved(own, "col", col_xor(1))
    factor, inverse = corner_call(ids, own, other)

    marks = arrived[:, T, 0].astype(jnp.int32)
    sums = combine_call(marks, arrived)
    next_front = [(f, (f + 1) % 4) for f in range(4)]
    first = moved(sums[0], "front", next_front)
    second = moved(sums[1], "front", next_front)
    body_rows = (2 + jnp.arange(6)) * ROWS + r
    padded0 = masked(stored[0, 2:] + first, body_rows[:, None, None], c)
    padded1 = masked(stored[1, 2:] + second, body_rows[:, None, None], c + COLS)
    gathered = lax.all_gather(padded0, "col", axis=0, tiled=False)[:NB]

    pick = jnp.stack([jnp.maximum(c // ROWS - 2, 0), c // ROWS + 2])
    chosen = jnp.take(gathered, pick, axis=1)
    right = jnp.where(r == c % ROWS, chosen, 0.0)
    for s in (1, 2, 3):
        pairs = [(i % ROWS * COLS + i, (i % ROWS + s) % ROWS * COLS + i) for i in range(COLS)]
        right = right + moved(chosen, ("row", "col"), pairs)

    lower, product = body_call(factor, inverse, gathered, right)

    product = product.reshape(6, T, 2, T)
    in_panel = c < NB
    at = jnp.minimum(c, NB - 1)
    panel_body = lax.dynamic_index_in_dim(lower, at, 0, keepdims=False)[: 6 * T].reshape(6, T, T)
    body0 = jnp.where(in_panel, panel_body, padded0 - product[:, :, 0])
    body1 = padded1 - product[:, :, 1]
    column = lax.dynamic_index_in_dim(factor, at, 0, keepdims=False).reshape(NB, T, T)
    head = lax.dynamic_slice_in_dim(column.reshape(2, ROWS, T, T), r, 1, axis=1)[:, 0]
    head0 = jnp.where(in_panel, head, 0.0)
    result0 = jnp.concatenate([head0, body0], 0)
    result1 = jnp.concatenate([jnp.zeros((2, T, T), jnp.float32), body1], 0)
    result = jnp.stack([result0, result1], 2)
    return result.reshape(front.shape)


def solution(mesh):
    spec = P("front", None, "row", None, None, "col", None)
    placed = (
        spec,
        P("front", ("row", "col"), None, None),
        P("front", ("row", "col"), None),
        P("front", ("row", "col")),
        P("front", ("row", "col")),
        P("front"),
    )
    return jax.shard_map(on_device, mesh=mesh, in_specs=placed, out_specs=spec, check_vma=False)
```

```python
import jax
import jax.numpy as jnp
from jax import lax
from jax.experimental import pallas as pl
from jax.experimental.pallas import tpu as pltpu
from jax.sharding import PartitionSpec as P

T = 128
G = 8
NB = 8
ROWS = 4
COLS = 16
VMEM_LIMIT = 24 * 1024 * 1024


def params():
    return pltpu.CompilerParams(vmem_limit_bytes=VMEM_LIMIT)


def split(x):
    h = x.astype(jnp.bfloat16)
    x = x - h.astype(jnp.float32)
    m = x.astype(jnp.bfloat16)
    low = (x - m.astype(jnp.float32)).astype(jnp.bfloat16)
    return h, m, low


def left_terms(x, axis):
    h, m, low = split(x)
    return jnp.concatenate([h, h, m, h, low, m], axis)


def right_terms(x, axis):
    h, m, low = split(x)
    return jnp.concatenate([h, m, h, low, h, m], axis)


def dot_rows(a, b):
    return lax.dot_general(a, b, (((1,), (1,)), ((), ())), preferred_element_type=jnp.float32)


def dot_columns(a, b):
    return lax.dot_general(a, b, (((0,), (0,)), ((), ())), preferred_element_type=jnp.float32)


def factor_tile(s_ref, w_ref, spare):
    span = 32
    rows = lax.broadcasted_iota(jnp.int32, (T, T), 0)
    lanes = lax.broadcasted_iota(jnp.int32, (T, T), 1)
    w_ref[...] = (rows == lanes).astype(jnp.float32)
    sub = lax.broadcasted_iota(jnp.int32, (G, T), 0)
    lane = lax.broadcasted_iota(jnp.int32, (G, T), 1)
    count = span // G
    done = 0
    for base in range(0, T, span):
        left = [s_ref[base + G * g:base + G * (g + 1), :] for g in range(count)]
        right = [w_ref[base + G * g:base + G * (g + 1), :] for g in range(count)]
        for g in range(count):
            r0 = base + G * g
            R, W = left[g], right[g]
            e = [[None] * G for _ in range(G)]
            for t in range(G):
                column = jnp.broadcast_to(R[:, r0 + t:r0 + t + 1], (G, T))
                for s in range(t + 1):
                    e[s][t] = jnp.broadcast_to(column[s:s + 1, :], (G, T))
            a = [jnp.broadcast_to(R[t:t + 1, :], (G, T)) for t in range(G)]
            w = [jnp.broadcast_to(W[t:t + 1, :], (G, T)) for t in range(G)]
            c = {
                i: [jnp.broadcast_to(left[i][:, r0 + t:r0 + t + 1], (G, T)) for t in range(G)]
                for i in range(g + 1, count)
            }
            U = jnp.zeros((G, T), jnp.float32)
            X = jnp.zeros((G, T), jnp.float32)
            for t in range(G):
                rec = 1.0 / e[t][t]
                root = lax.rsqrt(e[t][t])
                m = {}
                for s in range(t + 1, G):
                    m[s] = e[t][s] * rec
                    for q in range(s, G):
                        if s == t + 1 and q == s:
                            e[s][q] = e[s][q] - (e[t][s] * e[t][q]) * rec
                        else:
                            e[s][q] = e[s][q] - m[s] * e[t][q]
                for s in range(t + 1, G):
                    a[s] = a[s] - m[s] * a[t]
                    w[s] = w[s] - m[s] * w[t]
                U = jnp.where(sub == t, a[t] * root, U)
                X = jnp.where(sub == t, w[t] * root, X)
                for i in range(g + 1, count):
                    for s in range(t + 1, G):
                        c[i][s] = c[i][s] - m[s] * c[i][t]
                    ct = c[i][t] * rec
                    left[i] = left[i] - ct * a[t]
                    right[i] = right[i] - ct * w[t]
            left[g] = jnp.where(lane >= r0 + sub, U, 0.0)
            right[g] = X
            step = (base + G * g) // G + 1
            while done * (T // G) < len(spare) * step:
                spare[done]()
                done += 1
        U = jnp.concatenate(left, 0)
        X = jnp.concatenate(right, 0)
        s_ref[base:base + span, :] = U
        w_ref[base:base + span, :] = X
        end = base + span
        if end < T:
            prod = dot_columns(left_terms(U, 0), right_terms(jnp.concatenate([U, X], 1), 0))
            s_ref[end:, :] = s_ref[end:, :] - prod[end:, :T]
            w_ref[end:, :] = w_ref[end:, :] - prod[end:, T:]


CUTS = (0, 3, 6, 8)


def home(j):
    return j // 2 if j % 2 == 0 else NB - 1 - j // 2


def row_work(before, first, done_ref, w_ref, x_ref, parts_ref, left_ref, terms_ref, solved_ref):
    seen = set()

    def get(j):
        if j not in seen:
            return x_ref[home(j)] if before == 0 else x_ref[j - before]
        return solved_ref[j - before] if j < first else left_ref[j - first]

    def put(j, value):
        seen.add(j)
        if j < first:
            solved_ref[j - before] = value
        else:
            left_ref[j - first] = value

    def solve(k):
        x = dot_rows(left_terms(get(k), 1), right_terms(w_ref[k - before], 1))
        put(k, x)
        h, m, low = split(x)
        terms_ref[:, 6 * T * (k - before):6 * T * (k - before + 1)] = jnp.concatenate([h, h, m, h, low, m], 1)
        parts_ref[:, 2 * T * (k - before):2 * T * (k - before + 1)] = jnp.concatenate([h, m], 1)

    def update(k, j, hi):
        terms = terms_ref[:, 6 * T * (k - before):6 * T * (k - before + 1)]
        d = dot_rows(terms, right_terms(done_ref[k - before, (j - before) * T:(hi - before) * T, :], 1))
        for i in range(j, hi):
            put(i, get(i) - d[:, (i - j) * T:(i - j + 1) * T])

    work = []
    for k in range(before, first):
        work.append(lambda k=k: solve(k))
        for j in range(k + 1, NB, 2):
            work.append(lambda k=k, j=j: update(k, j, min(j + 2, NB)))
    return work


def corner_part(first, last, refs):
    ids_ref = refs[0]
    others = []
    if first == 0:
        own_ref, other_ref, own_far_ref, other_far_ref = refs[1:5]
        done_ref, w_ref, rest_ref, s_ref, xl_ref, xr_ref = refs[5:]
    else:
        before = CUTS[CUTS.index(first) - 1]
        state_ref, old_ref, old_w_ref, x_ref = refs[1:5]
        s_ref, xl_ref, xr_ref, terms_ref, solved_ref = refs[-5:]
        if last < NB:
            done_ref, w_ref, rest_ref, parts_ref, column_ref, left_ref = refs[5:-5]
        else:
            done_ref, w_ref, parts_ref, column_ref, left_ref = refs[5:-5]
        others = row_work(before, first, old_ref, old_w_ref, x_ref, parts_ref, left_ref, terms_ref, solved_ref)

    def put(j, lo, hi, value):
        if j < last:
            done_ref[j - first, (lo - first) * T:(hi - first) * T, :] = value
        else:
            rest_ref[j - last, (lo - last) * T:(hi - last) * T, :] = value

    def get(j, lo, hi):
        if j < last:
            return done_ref[j - first, (lo - first) * T:(hi - first) * T, :]
        return rest_ref[j - last, (lo - last) * T:(hi - last) * T, :]

    rows = lax.broadcasted_iota(jnp.int32, (T, T), 0)
    lanes = lax.broadcasted_iota(jnp.int32, (T, T), 1)
    if first == 0:
        z = ids_ref[0]
        h = ids_ref[1]
        r = ids_ref[2]
        for j in range(NB):
            s = (z + NB - home(j)) % NB
            for i in range(j, NB):
                t = (r + NB - i) % ROWS
                near = jnp.where(s > 4, s - 1, jnp.minimum(s, 3))
                value = jnp.where(
                    s == 4,
                    jnp.where(h == i // ROWS, own_far_ref[t], other_far_ref[t]),
                    jnp.where(h == i // ROWS, own_ref[near, t], other_ref[near, t]),
                )
                if i == j:
                    low = jnp.where(rows >= lanes, value, 0.0)
                    value = low + jnp.where(rows > lanes, value, 0.0).T
                put(j, i, i + 1, value)
    else:
        for j in range(first, NB):
            put(j, j, NB, state_ref[j - first, (j - first) * T:, :])
    for j in range(first + 1, last):
        done_ref[j - first, :(j - first) * T, :] = jnp.zeros(((j - first) * T, T), jnp.float32)

    def panel(k, lo, hi):
        x = dot_rows(left_terms(get(k, lo, hi), 1), right_terms(w_ref[k - first], 1))
        put(k, lo, hi, x)
        xl_ref[lo * T:hi * T, :] = left_terms(x, 1)
        xr_ref[lo * T:hi * T, :] = right_terms(x, 1)

    def trail(j, lo):
        put(j, lo, NB, get(j, lo, NB) - dot_rows(xl_ref[lo * T:, :], xr_ref[j * T:(j + 1) * T, :]))

    def trail_pair(j):
        d = dot_rows(xl_ref[j * T:, :], xr_ref[j * T:(j + 2) * T, :])
        put(j, j, NB, get(j, j, NB) - d[:, :T])
        put(j + 1, j + 1, NB, get(j + 1, j + 1, NB) - d[T:, T:])

    spare = []
    s_ref[...] = get(first, first, first + 1)
    for k in range(first, last):
        count = -(-len(others) // (last - k))
        spare, others = spare + others[:count], others[count:]
        factor_tile(s_ref, w_ref.at[k - first], spare)
        put(k, k, k + 1, s_ref[...].T)
        if k == NB - 1:
            break
        n = k + 1
        panel(k, n, n + 1)
        spare = []
        if n < last:
            s_ref[...] = get(n, n, n + 1) - dot_rows(xl_ref[n * T:(n + 1) * T, :], xr_ref[n * T:(n + 1) * T, :])
        else:
            spare.append(lambda n=n: trail(n, n))
        if n + 1 < NB:
            spare.append(lambda k=k, n=n: panel(k, n + 1, NB))
            if n < last:
                spare.append(lambda n=n: trail(n, n + 1))
            else:
                spare = spare[1:] + spare[:1]
            for j in range(n + 1, NB, 2):
                if j + 1 < NB:
                    spare.append(lambda j=j: trail_pair(j))
                else:
                    spare.append(lambda j=j: trail(j, j))
        if n == last:
            for work in spare:
                work()
    if first > 0:
        column_ref[...] = solved_ref[jnp.clip(ids_ref[3] - before, 0, first - before - 1)]


def corner_call(part, ids, *state):
    first, last = CUTS[part], CUTS[part + 1]
    smem = pl.BlockSpec(memory_space=pltpu.SMEM)
    vmem = pl.BlockSpec(memory_space=pltpu.VMEM)
    span = (NB - first) * T
    shapes = [
        jax.ShapeDtypeStruct((last - first, span, T), jnp.float32),
        jax.ShapeDtypeStruct((last - first, T, T), jnp.float32),
    ]
    extra = []
    if last < NB:
        shapes.append(jax.ShapeDtypeStruct((NB - last, (NB - last) * T, T), jnp.float32))
    if first > 0:
        width = first - CUTS[part - 1]
        shapes.append(jax.ShapeDtypeStruct((6 * T, 2 * T * width), jnp.bfloat16))
        shapes.append(jax.ShapeDtypeStruct((6 * T, T), jnp.float32))
        shapes.append(jax.ShapeDtypeStruct((NB - first, 6 * T, T), jnp.float32))
        extra = [pltpu.VMEM((6 * T, 6 * T * width), jnp.bfloat16), pltpu.VMEM((width, 6 * T, T), jnp.float32)]

    def kernel(*refs):
        corner_part(first, last, refs)

    return pl.pallas_call(
        kernel,
        in_specs=[smem] + [vmem] * len(state),
        out_specs=[vmem] * len(shapes),
        out_shape=shapes,
        scratch_shapes=[
            pltpu.VMEM((T, T), jnp.float32),
            pltpu.VMEM((NB * T, 6 * T), jnp.bfloat16),
            pltpu.VMEM((NB * T, 6 * T), jnp.bfloat16),
            *extra,
        ],
        compiler_params=params(),
    )(ids, *state)


def last_kernel(*refs):
    ids_ref, mark_ref = refs[:2]
    done_refs, w_refs, sent_refs = refs[2:5], refs[5:8], refs[8:12]
    parts0_ref, parts1_ref, column0_ref, column1_ref, left_ref, front_ref, tiles_ref = refs[12:19]
    out_ref, x_ref, xa_ref, xb_ref, pad_ref = refs[19:]
    r = ids_ref[2]
    c = ids_ref[3]
    which = (r + ROWS - c % ROWS) % ROWS
    for s, ref in enumerate(sent_refs):
        @pl.when(which == s)
        def _(ref=ref):
            for k in range(NB):
                x_ref[k, :2 * T] = ref[home(k)].reshape(2 * T, T)

    for b in range(2):
        pad_ref[b] = front_ref[b, 2:]

    def add_tile(s, carry):
        mark = mark_ref[s] - 1

        @pl.when(mark >= 0)
        def _():
            b = mark // 8
            a = mark % 8 - 2
            pad_ref[b, a] = pad_ref[b, a] + tiles_ref[s, :T, :]

        return carry

    lax.fori_loop(0, 2 * COLS, add_tile, 0)
    rows = 8 * T
    for k in (6, 7):
        x_ref[k, 2 * T:] = left_ref[k - 6]
    for k in range(NB):
        part = sum(k >= cut for cut in CUTS[1:-1])
        first = CUTS[part]
        done_ref, w_ref = done_refs[part], w_refs[part]
        high = rows if k >= 6 else 2 * T
        x = dot_rows(left_terms(x_ref[k, :high], 1), right_terms(w_ref[k - first], 1))
        x_ref[k, :high] = x
        h, m, low = split(x)
        xb_ref[:, 3 * T * k:3 * T * (k + 1)] = jnp.concatenate([h, m, h], 1)[:2 * T]
        terms = jnp.concatenate([h, h, m, h, low, m], 1)
        if k >= 6:
            xa_ref[:, 3 * T * (k - 6):3 * T * (k - 5)] = terms[2 * T:, :3 * T]
        for j in range(k + 1, NB, 2):
            hi = min(j + 2, NB)
            d = dot_rows(terms, right_terms(done_ref[k - first, (j - first) * T:(hi - first) * T, :], 1))
            for i in range(j, hi):
                x_ref[i, :high] = x_ref[i, :high] - d[:, (i - j) * T:(i - j + 1) * T]
    pieces = []
    for ref in (parts0_ref, parts1_ref):
        for k in range(3):
            h = ref[:, 2 * T * k:2 * T * k + T]
            pieces += [h, ref[:, 2 * T * k:2 * T * (k + 1)]]
    product = dot_rows(jnp.concatenate(pieces + [xa_ref[...]], 1), xb_ref[...])
    limit = ids_ref[4]
    lower = lax.broadcasted_iota(jnp.int32, (T, T), 0)
    lanes = lax.broadcasted_iota(jnp.int32, (T, T), 1)

    def padded(b):
        j = (b * COLS + c) * T + lanes
        tiles = []
        for a in range(6):
            i = ((a + 2) * ROWS + r) * T + lower
            unit = jnp.where(i == j, 1.0, 0.0)
            tiles.append(jnp.where(jnp.logical_and(i < limit, j < limit), pad_ref[b, a], unit))
        return jnp.concatenate(tiles, 0)

    in_panel = c < NB
    zeros = jnp.zeros((2 * T, T), jnp.float32)
    out_ref[pl.Slice(0, 2 * T, 2), :] = zeros
    out_ref[pl.Slice(1, 2 * T, 2), :] = zeros
    out_ref[pl.Slice(4 * T + 1, 6 * T, 2), :] = padded(1) - product[:, T:]

    @pl.when(jnp.logical_not(in_panel))
    def _():
        out_ref[pl.Slice(4 * T, 6 * T, 2), :] = padded(0) - product[:, :T]

    @pl.when(c < 3)
    def _():
        out_ref[pl.Slice(4 * T, 6 * T, 2), :] = column0_ref[...]

    @pl.when(jnp.logical_and(c >= 3, c < 6))
    def _():
        out_ref[pl.Slice(4 * T, 6 * T, 2), :] = column1_ref[...]

    @pl.when(jnp.logical_and(c >= 6, c < 8))
    def _():
        out_ref[pl.Slice(4 * T, 6 * T, 2), :] = x_ref[jnp.clip(c, 6, 7), 2 * T:]

    for a in range(2):
        i = r + ROWS * a
        for part, ref in enumerate(done_refs):
            first, last = CUTS[part], CUTS[part + 1]

            @pl.when(jnp.logical_and(jnp.logical_and(c >= first, c < last), i >= first))
            def _(ref=ref, first=first, last=last, a=a):
                at = pl.multiple_of(jnp.maximum(i - first, 0) * T, T)
                out_ref[pl.Slice(2 * a * T, T, 2), :] = ref[jnp.clip(c - first, 0, last - first - 1), pl.ds(at, T), :]


def last_call(ids, marks, parts, sent, front, tiles):
    smem = pl.BlockSpec(memory_space=pltpu.SMEM)
    vmem = pl.BlockSpec(memory_space=pltpu.VMEM)
    operands = [p[0] for p in parts] + [p[1] for p in parts] + list(sent)
    operands += [parts[1][-3], parts[2][-3], parts[1][-2], parts[2][-2], parts[2][-1], front, tiles]
    return pl.pallas_call(
        last_kernel,
        in_specs=[smem, smem] + [vmem] * len(operands),
        out_specs=vmem,
        out_shape=jax.ShapeDtypeStruct((16 * T, T), jnp.float32),
        scratch_shapes=[
            pltpu.VMEM((NB, NB * T, T), jnp.float32),
            pltpu.VMEM((6 * T, 6 * T), jnp.bfloat16),
            pltpu.VMEM((2 * T, 3 * T * NB), jnp.bfloat16),
            pltpu.VMEM((2, 6, T, T), jnp.float32),
        ],
        compiler_params=params(),
    )(ids, marks, *operands)


def scatter_kernel(ids_ref, owner_ref, row_ref, col_ref, tiles_ref, dense_ref, raw_ref):
    z = ids_ref[0]
    h = ids_ref[1]
    dense_ref[...] = jnp.zeros(dense_ref.shape, jnp.float32)

    def step(i, carry):
        o = owner_ref[i]
        a = row_ref[i]
        b = col_ref[i]
        panel = jnp.logical_and(b == 0, o < NB)

        @pl.when(panel)
        def _():
            core = jnp.where(a < 2, a, (a - 2) // 3)
            place = jnp.where(a < 2, 0, a - 1 - 3 * core)
            q = jnp.bitwise_xor(core, h)
            p = (jnp.where(o % 2 == 0, o // 2, NB - 1 - o // 2) + NB - z) % NB
            dense_ref[q, p, place] = dense_ref[q, p, place] + tiles_ref[i]

        mark = jnp.where(jnp.logical_or(panel, a < 2), 0, o * 16 + b * 8 + a + 1)
        raw_ref[i, :T, :] = tiles_ref[i]
        raw_ref[i, T:, :] = jnp.full((8, T), mark.astype(jnp.float32), jnp.float32)
        return carry

    lax.fori_loop(0, owner_ref.shape[0], step, 0)


def scatter_call(ids, owner, row, col, tiles):
    smem = pl.BlockSpec(memory_space=pltpu.SMEM)
    vmem = pl.BlockSpec(memory_space=pltpu.VMEM)
    return pl.pallas_call(
        scatter_kernel,
        in_specs=[smem, smem, smem, smem, vmem],
        out_specs=[vmem, vmem],
        out_shape=[
            jax.ShapeDtypeStruct((2, NB, 4, T, T), jnp.float32),
            jax.ShapeDtypeStruct((COLS, T + 8, T), jnp.float32),
        ],
        compiler_params=params(),
    )(ids, owner, row, col, tiles)


def slot_kernel(mark_ref, raw0_ref, raw1_ref, raw2_ref, send_ref, count_ref):
    for o in range(COLS):
        send_ref[2 * o, T:, :] = jnp.zeros((8, T), jnp.float32)
        send_ref[2 * o + 1, T:, :] = jnp.zeros((8, T), jnp.float32)
        count_ref[o] = 0

    start = 0
    for ref in (raw0_ref, raw1_ref, raw2_ref):

        def step(i, carry, ref=ref, start=start):
            mark = mark_ref[start + i] - 1

            @pl.when(mark >= 0)
            def _():
                o = mark // 16
                slot = 2 * o + count_ref[o]
                count_ref[o] = count_ref[o] + 1
                send_ref[slot, :T, :] = ref[i, :T, :]
                send_ref[slot, T:, :] = jnp.full((8, T), (mark % 16 + 1).astype(jnp.float32), jnp.float32)

            return carry

        lax.fori_loop(0, ref.shape[0], step, 0)
        start += ref.shape[0]


def slot_call(marks, *raw):
    smem = pl.BlockSpec(memory_space=pltpu.SMEM)
    vmem = pl.BlockSpec(memory_space=pltpu.VMEM)
    return pl.pallas_call(
        slot_kernel,
        in_specs=[smem, vmem, vmem, vmem],
        out_specs=vmem,
        out_shape=jax.ShapeDtypeStruct((2 * COLS, T + 8, T), jnp.float32),
        scratch_shapes=[pltpu.SMEM((COLS,), jnp.int32)],
        compiler_params=params(),
    )(marks, *raw)


def moved(value, axes, pairs):
    return lax.ppermute(value, axes, pairs)


def together(*values):
    return lax.optimization_barrier(values)


def after(value, *others):
    return lax.optimization_barrier((value, *others))[0]


def on_device(front, child_tiles, child_owner, child_row, child_col, front_size):
    r = lax.axis_index("row")
    c = lax.axis_index("col")
    z = c // 2
    h = c % 2
    limit = front_size[0]
    stored = front.reshape(8, T, 2, T).transpose(2, 0, 1, 3)
    ids = jnp.stack([z, h, r, c, limit]).astype(jnp.int32)
    next_front = [(f, (f + 1) % 4) for f in range(4)]
    ahead_one = [(i, (i + 2) % COLS) for i in range(COLS)]
    behind_one = [(i, (i - 2) % COLS) for i in range(COLS)]
    swap = [(i, i ^ 1) for i in range(COLS)]
    both_axes = ("front", "col")
    hop = [(f * COLS + i, (f + 1) % 4 * COLS + i) for f in range(4) for i in range(COLS)]
    hop_ahead = [(f * COLS + i, (f + 1) % 4 * COLS + (i + 2) % COLS) for f in range(4) for i in range(COLS)]

    dense, raw = scatter_call(ids, child_owner[0, :, 0], child_row[0], child_col[0], child_tiles[0])

    first = jnp.concatenate([stored[0, :1], stored[0, 2:5]], 0)
    second = jnp.concatenate([stored[0, 1:2], stored[0, 5:]], 0)
    even = moved(first, "col", [(j, 2 * home(j)) for j in range(NB)])
    odd = moved(second, "col", [(j, 2 * home(j) + 1) for j in range(NB)])

    chunk = dense[0] + moved(dense[1], "col", swap)
    raw_parts = []
    up = chunk[4]
    down = chunk[5]
    for s, t in ((3, 6), (2, 7), (1, 0)):
        lo, hi = {3: (0, 5), 2: (5, 11), 1: (11, 16)}[s]
        up, down, piece = together(
            moved(up, "col", ahead_one), moved(down, "col", behind_one), moved(raw[lo:hi], "front", next_front)
        )
        raw_parts.append(piece)
        if s == 2:
            up, down, even = together(up, down, even)
        if s == 1:
            up, down, odd = together(up, down, odd)
        up = chunk[s] + up
        down = chunk[t] + down
    mine = jnp.where(h == 0, even, odd)
    corner = mine[:1] + moved(down[:1], both_axes, hop) + moved(up[:1], both_axes, hop_ahead)

    quad = jnp.concatenate(
        [corner] + [moved(corner, "row", [(i, (i + s) % ROWS) for i in range(ROWS)]) for s in (1, 2, 3)], 0
    )

    body = mine[1:] + moved(down[1:], both_axes, hop) + moved(up[1:], both_axes, hop_ahead)
    half_rows = ((2 + 3 * h + jnp.arange(3)) * ROWS + r)[:, None, None]
    body = jnp.where(half_rows * T + jnp.arange(T)[:, None] < limit, body, 0.0)
    gathered = lax.all_gather(body, "col", axis=0, tiled=False).reshape(NB, 6, T, T)

    pieces = {0: quad}
    ahead = behind = quad
    for s in (1, 2, 3):
        ahead, behind = together(moved(ahead, "col", ahead_one), moved(behind, "col", behind_one))
        pieces[s] = ahead
        pieces[NB - s] = behind
    own = jnp.stack([pieces[s] for s in sorted(pieces)])
    far, other = together(moved(ahead, "col", ahead_one), moved(own, "col", swap))
    other_far = moved(far, "col", swap)

    raw_parts = after(raw_parts, quad)
    raw_marks = jnp.concatenate([piece[:, T, 0] for piece in raw_parts]).astype(jnp.int32)
    send = slot_call(raw_marks, *raw_parts)
    arrived = lax.all_to_all(after(send, far), "col", split_axis=0, concat_axis=0, tiled=True)
    part0 = corner_call(0, after(ids, body), own, other, far, other_far)

    first_done = part0[1]

    pick = [jnp.maximum(c // ROWS - 2, 0), c // ROWS + 2]
    gathered = after(gathered, first_done)
    chosen = jnp.concatenate([lax.dynamic_slice_in_dim(gathered, p, 1, axis=1) for p in pick], 1)
    sent = [chosen]
    for s in (1, 2, 3):
        pairs = [(i % ROWS * COLS + i, (i % ROWS + s) % ROWS * COLS + i) for i in range(COLS)]
        sent.append(moved(chosen, ("row", "col"), pairs))
    part1 = corner_call(1, after(ids, chosen), part0[2], part0[0], part0[1], gathered.reshape(NB, 6 * T, T))
    part2 = corner_call(2, ids, part1[2], part1[0], part1[1], part1[-1])
    parts = (part0, part1, part2)

    arrived = after(arrived, part1[1])
    marks = arrived[:, T, 0].astype(jnp.int32)
    result = last_call(ids, marks, parts, sent, stored, arrived)
    return result.reshape(front.shape)


def solution(mesh):
    spec = P("front", None, "row", None, None, "col", None)
    placed = (
        spec,
        P("front", ("row", "col"), None, None),
        P("front", ("row", "col"), None),
        P("front", ("row", "col")),
        P("front", ("row", "col")),
        P("front"),
    )
    return jax.shard_map(on_device, mesh=mesh, in_specs=placed, out_specs=spec, check_vma=False)
```

```python
import jax
import jax.numpy as jnp
from jax import lax
from jax.experimental import pallas as pl
from jax.experimental.pallas import tpu as pltpu
from jax.sharding import PartitionSpec as P

T = 128
G = 8
NB = 8
ROWS = 4
COLS = 16
VMEM_LIMIT = 60 * 1024 * 1024


def params():
    return pltpu.CompilerParams(vmem_limit_bytes=VMEM_LIMIT)


def split(x):
    h = x.astype(jnp.bfloat16)
    x = x - h.astype(jnp.float32)
    m = x.astype(jnp.bfloat16)
    low = (x - m.astype(jnp.float32)).astype(jnp.bfloat16)
    return h, m, low


def left_terms(x, axis):
    h, m, low = split(x)
    return jnp.concatenate([h, h, m, h, low, m], axis)


def right_terms(x, axis):
    h, m, low = split(x)
    return jnp.concatenate([h, m, h, low, h, m], axis)


def short_left(x):
    h, m, low = split(x)
    return jnp.concatenate([h, h, m], 1)


def short_right(x):
    h, m, low = split(x)
    return jnp.concatenate([h, m, h], 1)


def dot_rows(a, b):
    return lax.dot_general(a, b, (((1,), (1,)), ((), ())), preferred_element_type=jnp.float32)


def dot_columns(a, b):
    return lax.dot_general(a, b, (((0,), (0,)), ((), ())), preferred_element_type=jnp.float32)


def factor_tile(s_ref, w_ref, spare):
    span = 32
    rows = lax.broadcasted_iota(jnp.int32, (T, T), 0)
    lanes = lax.broadcasted_iota(jnp.int32, (T, T), 1)
    w_ref[...] = (rows == lanes).astype(jnp.float32)
    sub = lax.broadcasted_iota(jnp.int32, (G, T), 0)
    lane = lax.broadcasted_iota(jnp.int32, (G, T), 1)
    count = span // G
    done = 0
    for base in range(0, T, span):
        left = [s_ref[base + G * g:base + G * (g + 1), :] for g in range(count)]
        right = [w_ref[base + G * g:base + G * (g + 1), :] for g in range(count)]
        for g in range(count):
            r0 = base + G * g
            R, W = left[g], right[g]
            e = [[None] * G for _ in range(G)]
            for t in range(G):
                column = jnp.broadcast_to(R[:, r0 + t:r0 + t + 1], (G, T))
                for s in range(t + 1):
                    e[s][t] = jnp.broadcast_to(column[s:s + 1, :], (G, T))
            a = [jnp.broadcast_to(R[t:t + 1, :], (G, T)) for t in range(G)]
            w = [jnp.broadcast_to(W[t:t + 1, :], (G, T)) for t in range(G)]
            c = {
                i: [jnp.broadcast_to(left[i][:, r0 + t:r0 + t + 1], (G, T)) for t in range(G)]
                for i in range(g + 1, count)
            }
            U = jnp.zeros((G, T), jnp.float32)
            X = jnp.zeros((G, T), jnp.float32)
            for t in range(G):
                rec = 1.0 / e[t][t]
                root = lax.rsqrt(e[t][t])
                m = {}
                for s in range(t + 1, G):
                    m[s] = e[t][s] * rec
                    for q in range(s, G):
                        if s == t + 1 and q == s:
                            e[s][q] = e[s][q] - (e[t][s] * e[t][q]) * rec
                        else:
                            e[s][q] = e[s][q] - m[s] * e[t][q]
                for s in range(t + 1, G):
                    a[s] = a[s] - m[s] * a[t]
                    w[s] = w[s] - m[s] * w[t]
                U = jnp.where(sub == t, a[t] * root, U)
                X = jnp.where(sub == t, w[t] * root, X)
                for i in range(g + 1, count):
                    for s in range(t + 1, G):
                        c[i][s] = c[i][s] - m[s] * c[i][t]
                    ct = c[i][t] * rec
                    left[i] = left[i] - ct * a[t]
                    right[i] = right[i] - ct * w[t]
            left[g] = jnp.where(lane >= r0 + sub, U, 0.0)
            right[g] = X
            step = (base + G * g) // G + 1
            while done * (T // G) < len(spare) * step:
                spare[done]()
                done += 1
        U = jnp.concatenate(left, 0)
        X = jnp.concatenate(right, 0)
        s_ref[base:base + span, :] = U
        w_ref[base:base + span, :] = X
        end = base + span
        if end < T:
            prod = dot_columns(left_terms(U, 0), right_terms(jnp.concatenate([U, X], 1), 0))
            s_ref[end:, :] = s_ref[end:, :] - prod[end:, :T]
            w_ref[end:, :] = w_ref[end:, :] - prod[end:, T:]


CUTS = (0, 3, 6, 8)


def home(j):
    return j // 2 if j % 2 == 0 else NB - 1 - j // 2


def row_work(before, first, done_ref, w_ref, x_ref, parts_ref, left_ref, terms_ref, solved_ref):
    seen = set()

    def get(j):
        if j not in seen:
            return x_ref[home(j)] if before == 0 else x_ref[j - before]
        return solved_ref[j - before] if j < first else left_ref[j - first]

    def put(j, value):
        seen.add(j)
        if j < first:
            solved_ref[j - before] = value
        else:
            left_ref[j - first] = value

    def solve(k):
        x = dot_rows(short_left(get(k)), short_right(w_ref[k - before]))
        put(k, x)
        terms_ref[:, 3 * T * (k - before):3 * T * (k - before + 1)] = short_left(x)
        parts_ref[:, 2 * T * (k - before):2 * T * (k - before + 1)] = short_left(x)[:, T:]

    def update(k, j, hi):
        terms = terms_ref[:, 3 * T * (k - before):3 * T * (k - before + 1)]
        d = dot_rows(terms, short_right(done_ref[k - before, (j - before) * T:(hi - before) * T, :]))
        for i in range(j, hi):
            put(i, get(i) - d[:, (i - j) * T:(i - j + 1) * T])

    work = []
    for k in range(before, first):
        work.append(lambda k=k: solve(k))
        for j in range(k + 1, NB, 2):
            work.append(lambda k=k, j=j: update(k, j, min(j + 2, NB)))
    return work


def fetch(source, target, sem):
    copy = pltpu.make_async_copy(source, target, sem)
    copy.start()
    return copy


def corner_part(first, last, refs):
    ids_ref = refs[0]
    others = []
    inputs = 4
    ins, refs = refs[1:1 + inputs], refs[1 + inputs:]
    count = 2 + (last < NB) + 3 * (first > 0)
    outs, refs = refs[:count], refs[count:]
    held, refs = refs[:count], refs[count:]
    done_ref, w_ref = held[:2]
    rest_ref = held[2] if last < NB else None
    s_ref, xl_ref, xr_ref, in_sems, out_sems = refs[:5]
    refs = refs[5:]
    sent = []

    def store(source, target):
        sent.append(fetch(source, target, out_sems.at[len(sent)]))

    def put(j, lo, hi, value):
        if j < last:
            done_ref[j - first, (lo - first) * T:(hi - first) * T, :] = value
        else:
            rest_ref[j - last, (lo - last) * T:(hi - last) * T, :] = value

    def get(j, lo, hi):
        if j < last:
            return done_ref[j - first, (lo - first) * T:(hi - first) * T, :]
        return rest_ref[j - last, (lo - last) * T:(hi - last) * T, :]

    rows = lax.broadcasted_iota(jnp.int32, (T, T), 0)
    lanes = lax.broadcasted_iota(jnp.int32, (T, T), 1)
    if first == 0:
        own_ref, other_ref, own_far_ref, other_far_ref = refs
        z = ids_ref[0]
        h = ids_ref[1]
        r = ids_ref[2]
        copies = [fetch(ins[n], refs[n], in_sems.at[n]) for n in range(inputs)]
        for copy in copies:
            copy.wait()
        for j in range(NB):
            s = (z + NB - home(j)) % NB
            for i in range(j, NB):
                t = (r + NB - i) % ROWS
                near = jnp.where(s > 4, s - 1, jnp.minimum(s, 3))
                value = jnp.where(
                    s == 4,
                    jnp.where(h == i // ROWS, own_far_ref[t], other_far_ref[t]),
                    jnp.where(h == i // ROWS, own_ref[near, t], other_ref[near, t]),
                )
                if i == j:
                    low = jnp.where(rows >= lanes, value, 0.0)
                    value = low + jnp.where(rows > lanes, value, 0.0).T
                put(j, i, i + 1, value)
    else:
        before = CUTS[CUTS.index(first) - 1]
        state_ref, old_ref, old_w_ref, x_ref, terms_ref, solved_ref = refs
        parts_ref, column_ref, left_ref = held[-3:]
        late = []
        early = fetch(ins[0], state_ref, in_sems.at[0])
        for n, ref in ((1, old_ref), (2, old_w_ref), (3, x_ref)):
            late.append(fetch(ins[n], ref, in_sems.at[n]))

        def arrive():
            for copy in late:
                copy.wait()

        others = [arrive] + row_work(before, first, old_ref, old_w_ref, x_ref, parts_ref, left_ref, terms_ref, solved_ref)
        early.wait()
        for j in range(first, NB):
            put(j, j, NB, state_ref[j - first, (j - first) * T:, :])
    for j in range(first + 1, last):
        done_ref[j - first, :(j - first) * T, :] = jnp.zeros(((j - first) * T, T), jnp.float32)

    def panel(k, lo, hi):
        x = dot_rows(left_terms(get(k, lo, hi), 1), right_terms(w_ref[k - first], 1))
        put(k, lo, hi, x)
        xl_ref[lo * T:hi * T, :] = left_terms(x, 1)
        xr_ref[lo * T:hi * T, :] = right_terms(x, 1)

    def trail(j, lo):
        put(j, lo, NB, get(j, lo, NB) - dot_rows(xl_ref[lo * T:, :], xr_ref[j * T:(j + 1) * T, :]))

    def trail_pair(j):
        d = dot_rows(xl_ref[j * T:, :], xr_ref[j * T:(j + 2) * T, :])
        put(j, j, NB, get(j, j, NB) - d[:, :T])
        put(j + 1, j + 1, NB, get(j + 1, j + 1, NB) - d[T:, T:])

    spare = []
    s_ref[...] = get(first, first, first + 1)
    for k in range(first, last):
        share = -(-len(others) // (last - k))
        spare, others = spare + others[:share], others[share:]
        factor_tile(s_ref, w_ref.at[k - first], spare)
        put(k, k, k + 1, s_ref[...].T)
        if k > first:
            store(done_ref.at[k - 1 - first], outs[0].at[k - 1 - first])
        if k == NB - 1:
            break
        n = k + 1
        panel(k, n, n + 1)
        spare = []
        if n < last:
            s_ref[...] = get(n, n, n + 1) - dot_rows(xl_ref[n * T:(n + 1) * T, :], xr_ref[n * T:(n + 1) * T, :])
        else:
            spare.append(lambda n=n: trail(n, n))
        if n + 1 < NB:
            spare.append(lambda k=k, n=n: panel(k, n + 1, NB))
            if n < last:
                spare.append(lambda n=n: trail(n, n + 1))
            else:
                spare = spare[1:] + spare[:1]
            for j in range(n + 1, NB, 2):
                if j + 1 < NB:
                    spare.append(lambda j=j: trail_pair(j))
                else:
                    spare.append(lambda j=j: trail(j, j))
        if n == last:
            if first > 0:
                column_ref[...] = solved_ref[jnp.clip(ids_ref[3] - before, 0, first - before - 1)]
            for n in range(1, count):
                if n != 2:
                    store(held[n], outs[n])
            for work in spare:
                work()
    if last < NB:
        store(rest_ref, outs[2])
    else:
        column_ref[...] = solved_ref[jnp.clip(ids_ref[3] - before, 0, first - before - 1)]
        for n in range(1, count):
            store(held[n], outs[n])
    store(done_ref.at[last - 1 - first], outs[0].at[last - 1 - first])
    for copy in sent:
        copy.wait()


def corner_call(part, ids, *state):
    first, last = CUTS[part], CUTS[part + 1]
    smem = pl.BlockSpec(memory_space=pltpu.SMEM)
    far = pl.BlockSpec(memory_space=pl.ANY)
    span = (NB - first) * T
    shapes = [((last - first, span, T), jnp.float32), ((last - first, T, T), jnp.float32)]
    if last < NB:
        shapes.append(((NB - last, (NB - last) * T, T), jnp.float32))
    extra = [pltpu.VMEM(x.shape, x.dtype) for x in state]
    if first > 0:
        width = first - CUTS[part - 1]
        shapes.append(((6 * T, 2 * T * width), jnp.bfloat16))
        shapes.append(((6 * T, T), jnp.float32))
        shapes.append(((NB - first, 6 * T, T), jnp.float32))
        extra += [pltpu.VMEM((6 * T, 3 * T * width), jnp.bfloat16), pltpu.VMEM((width, 6 * T, T), jnp.float32)]

    def kernel(*refs):
        corner_part(first, last, refs)

    return pl.pallas_call(
        kernel,
        in_specs=[smem] + [far] * len(state),
        out_specs=[far] * len(shapes),
        out_shape=[jax.ShapeDtypeStruct(*x) for x in shapes],
        scratch_shapes=[pltpu.VMEM(*x) for x in shapes]
        + [
            pltpu.VMEM((T, T), jnp.float32),
            pltpu.VMEM((NB * T, 6 * T), jnp.bfloat16),
            pltpu.VMEM((NB * T, 6 * T), jnp.bfloat16),
            pltpu.SemaphoreType.DMA((len(state),)),
            pltpu.SemaphoreType.DMA((last - first + len(shapes) - 1,)),
            *extra,
        ],
        compiler_params=params(),
    )(ids, *state)


def last_kernel(*refs):
    ids_ref, mark_ref = refs[:2]
    ins, sent_in, column_in = refs[2:13], refs[13:17], refs[17:19]
    out_ref = refs[19]
    held = refs[20:31]
    done_refs, w_refs = held[:3], held[3:6]
    parts0_ref, parts1_ref, left_ref, front_ref, tiles_ref = held[6:]
    sent_ref, column_ref, x_ref, xa_ref, xb_ref, pad_ref, sems = refs[31:]
    r = ids_ref[2]
    c = ids_ref[3]
    which = (r + ROWS - c % ROWS) % ROWS
    for s, ref in enumerate(sent_in):
        @pl.when(which == s)
        def _(ref=ref):
            fetch(ref, sent_ref, sems.at[11])

    copies = [None] * 11
    for n in (0, 3, 8, 1, 4, 2, 5, 6, 7, 9, 10):
        copies[n] = fetch(ins[n], held[n], sems.at[n])
    pltpu.make_async_copy(sent_in[0], sent_ref, sems.at[11]).wait()
    for n in (0, 3, 8, 1, 4, 2, 5):
        copies[n].wait()
    for k in range(NB):
        x_ref[k, :2 * T] = sent_ref[home(k)].reshape(2 * T, T)

    rows = 8 * T
    for k in (6, 7):
        x_ref[k, 2 * T:] = left_ref[k - 6]
    for k in range(NB):
        part = sum(k >= cut for cut in CUTS[1:-1])
        first = CUTS[part]
        done_ref, w_ref = done_refs[part], w_refs[part]
        high = rows if k >= 6 else 2 * T
        x = dot_rows(short_left(x_ref[k, :high]), short_right(w_ref[k - first]))
        x_ref[k, :high] = x
        xb_ref[:, 3 * T * k:3 * T * (k + 1)] = short_right(x[:2 * T])
        terms = short_left(x)
        if k >= 6:
            xa_ref[:, 3 * T * (k - 6):3 * T * (k - 5)] = terms[2 * T:]
        for j in range(k + 1, NB, 2):
            hi = min(j + 2, NB)
            d = dot_rows(terms, short_right(done_ref[k - first, (j - first) * T:(hi - first) * T, :]))
            for i in range(j, hi):
                x_ref[i, :high] = x_ref[i, :high] - d[:, (i - j) * T:(i - j + 1) * T]
    for n in (6, 7, 9, 10):
        copies[n].wait()
    for b in range(2):
        pad_ref[b] = front_ref[b, 2:]

    def add_tile(s, carry):
        mark = mark_ref[s] - 1

        @pl.when(mark >= 0)
        def _():
            b = mark // 8
            a = mark % 8 - 2
            pad_ref[b, a] = pad_ref[b, a] + tiles_ref[s, :T, :]

        return carry

    lax.fori_loop(0, 2 * COLS, add_tile, 0)
    pieces = []
    for ref in (parts0_ref, parts1_ref):
        for k in range(3):
            h = ref[:, 2 * T * k:2 * T * k + T]
            pieces += [h, ref[:, 2 * T * k:2 * T * (k + 1)]]
    product = dot_rows(jnp.concatenate(pieces + [xa_ref[...]], 1), xb_ref[...])
    limit = ids_ref[4]
    lower = lax.broadcasted_iota(jnp.int32, (T, T), 0)
    lanes = lax.broadcasted_iota(jnp.int32, (T, T), 1)

    def padded(b):
        j = (b * COLS + c) * T + lanes
        tiles = []
        for a in range(6):
            i = ((a + 2) * ROWS + r) * T + lower
            unit = jnp.where(i == j, 1.0, 0.0)
            tiles.append(jnp.where(jnp.logical_and(i < limit, j < limit), pad_ref[b, a], unit))
        return jnp.concatenate(tiles, 0)

    in_panel = c < NB
    zeros = jnp.zeros((2 * T, T), jnp.float32)
    out_ref[pl.Slice(0, 2 * T, 2), :] = zeros
    out_ref[pl.Slice(1, 2 * T, 2), :] = zeros
    out_ref[pl.Slice(4 * T + 1, 6 * T, 2), :] = padded(1) - product[:, T:]

    @pl.when(jnp.logical_not(in_panel))
    def _():
        out_ref[pl.Slice(4 * T, 6 * T, 2), :] = padded(0) - product[:, :T]

    for n, ref in enumerate(column_in):
        @pl.when(jnp.logical_and(c >= CUTS[n], c < CUTS[n + 1]))
        def _(n=n, ref=ref):
            copy = fetch(ref, column_ref, sems.at[12])
            copy.wait()
            out_ref[pl.Slice(4 * T, 6 * T, 2), :] = column_ref[...]

    @pl.when(jnp.logical_and(c >= 6, c < 8))
    def _():
        out_ref[pl.Slice(4 * T, 6 * T, 2), :] = x_ref[jnp.clip(c, 6, 7), 2 * T:]

    for a in range(2):
        i = r + ROWS * a
        for part, ref in enumerate(done_refs):
            first, last = CUTS[part], CUTS[part + 1]

            @pl.when(jnp.logical_and(jnp.logical_and(c >= first, c < last), i >= first))
            def _(ref=ref, first=first, last=last, a=a):
                at = pl.multiple_of(jnp.maximum(i - first, 0) * T, T)
                out_ref[pl.Slice(2 * a * T, T, 2), :] = ref[jnp.clip(c - first, 0, last - first - 1), pl.ds(at, T), :]


def last_call(ids, marks, parts, sent, front, tiles):
    smem = pl.BlockSpec(memory_space=pltpu.SMEM)
    vmem = pl.BlockSpec(memory_space=pltpu.VMEM)
    far = pl.BlockSpec(memory_space=pl.ANY)
    operands = [p[0] for p in parts] + [p[1] for p in parts]
    operands += [parts[1][-3], parts[2][-3], parts[2][-1], front, tiles]
    others = list(sent) + [parts[1][-2], parts[2][-2]]
    return pl.pallas_call(
        last_kernel,
        in_specs=[smem, smem] + [far] * (len(operands) + len(others)),
        out_specs=vmem,
        out_shape=jax.ShapeDtypeStruct((16 * T, T), jnp.float32),
        scratch_shapes=[pltpu.VMEM(x.shape, x.dtype) for x in operands]
        + [
            pltpu.VMEM((NB, 2, T, T), jnp.float32),
            pltpu.VMEM((6 * T, T), jnp.float32),
            pltpu.VMEM((NB, NB * T, T), jnp.float32),
            pltpu.VMEM((6 * T, 6 * T), jnp.bfloat16),
            pltpu.VMEM((2 * T, 3 * T * NB), jnp.bfloat16),
            pltpu.VMEM((2, 6, T, T), jnp.float32),
            pltpu.SemaphoreType.DMA((13,)),
        ],
        compiler_params=params(),
    )(ids, marks, *operands, *others)


def scatter_kernel(ids_ref, owner_ref, row_ref, col_ref, tiles_ref, keep_ref, give_ref, raw_ref):
    z = ids_ref[0]
    h = ids_ref[1]
    keep_ref[...] = jnp.zeros(keep_ref.shape, jnp.float32)
    give_ref[...] = jnp.zeros(give_ref.shape, jnp.float32)

    def step(i, carry):
        o = owner_ref[i]
        a = row_ref[i]
        b = col_ref[i]
        panel = jnp.logical_and(b == 0, o < NB)

        @pl.when(panel)
        def _():
            core = jnp.where(a < 2, a, (a - 2) // 3)
            place = jnp.where(a < 2, 0, a - 1 - 3 * core)
            p = (jnp.where(o % 2 == 0, o // 2, NB - 1 - o // 2) + NB - z) % NB

            @pl.when(core == h)
            def _():
                keep_ref[p, place] = keep_ref[p, place] + tiles_ref[i]

            @pl.when(core != h)
            def _():
                give_ref[p, place] = give_ref[p, place] + tiles_ref[i]

        mark = jnp.where(jnp.logical_or(panel, a < 2), 0, o * 16 + b * 8 + a + 1)
        raw_ref[i, :T, :] = tiles_ref[i]
        raw_ref[i, T:, :] = jnp.full((8, T), mark.astype(jnp.float32), jnp.float32)
        return carry

    lax.fori_loop(0, owner_ref.shape[0], step, 0)


def scatter_call(ids, owner, row, col, tiles):
    smem = pl.BlockSpec(memory_space=pltpu.SMEM)
    vmem = pl.BlockSpec(memory_space=pltpu.VMEM)
    return pl.pallas_call(
        scatter_kernel,
        in_specs=[smem, smem, smem, smem, vmem],
        out_specs=[vmem, vmem, vmem],
        out_shape=[
            jax.ShapeDtypeStruct((NB, 4, T, T), jnp.float32),
            jax.ShapeDtypeStruct((NB, 4, T, T), jnp.float32),
            jax.ShapeDtypeStruct((COLS, T + 8, T), jnp.float32),
        ],
        compiler_params=params(),
    )(ids, owner, row, col, tiles)


def slot_kernel(mark_ref, raw_ref, send_ref, count_ref):
    for o in range(COLS):
        send_ref[2 * o, T:, :] = jnp.zeros((8, T), jnp.float32)
        send_ref[2 * o + 1, T:, :] = jnp.zeros((8, T), jnp.float32)
        count_ref[o] = 0

    def step(i, carry):
        mark = mark_ref[i] - 1

        @pl.when(mark >= 0)
        def _():
            o = mark // 16
            slot = 2 * o + count_ref[o]
            count_ref[o] = count_ref[o] + 1
            send_ref[slot, :T, :] = raw_ref[i, :T, :]
            send_ref[slot, T:, :] = jnp.full((8, T), (mark % 16 + 1).astype(jnp.float32), jnp.float32)

        return carry

    lax.fori_loop(0, COLS, step, 0)


def slot_call(marks, raw):
    smem = pl.BlockSpec(memory_space=pltpu.SMEM)
    vmem = pl.BlockSpec(memory_space=pltpu.VMEM)
    return pl.pallas_call(
        slot_kernel,
        in_specs=[smem, vmem],
        out_specs=vmem,
        out_shape=jax.ShapeDtypeStruct((2 * COLS, T + 8, T), jnp.float32),
        scratch_shapes=[pltpu.SMEM((COLS,), jnp.int32)],
        compiler_params=params(),
    )(marks, raw)


def moved(value, axes, pairs):
    return lax.ppermute(value, axes, pairs)


def together(*values):
    return lax.optimization_barrier(values)


def after(value, *others):
    return lax.optimization_barrier((value, *others))[0]


def on_device(front, child_tiles, child_owner, child_row, child_col, front_size):
    r = lax.axis_index("row")
    c = lax.axis_index("col")
    z = c // 2
    h = c % 2
    limit = front_size[0]
    stored = front.reshape(8, T, 2, T).transpose(2, 0, 1, 3)
    ids = jnp.stack([z, h, r, c, limit]).astype(jnp.int32)
    next_front = [(f, (f + 1) % 4) for f in range(4)]
    ahead_one = [(i, (i + 2) % COLS) for i in range(COLS)]
    behind_one = [(i, (i - 2) % COLS) for i in range(COLS)]
    swap = [(i, i ^ 1) for i in range(COLS)]
    both_axes = ("front", "col")
    hop = [(f * COLS + i, (f + 1) % 4 * COLS + i) for f in range(4) for i in range(COLS)]
    hop_ahead = [(f * COLS + i, (f + 1) % 4 * COLS + (i + 2) % COLS) for f in range(4) for i in range(COLS)]

    keep, give, raw = scatter_call(ids, child_owner[0, :, 0], child_row[0], child_col[0], child_tiles[0])

    to_even = [(j, 2 * home(j)) for j in range(NB)]
    to_odd = [(j, 2 * home(j) + 1) for j in range(NB)]
    corner_front = jnp.where(h == 0, moved(stored[0, :1], "col", to_even), moved(stored[0, 1:2], "col", to_odd))

    chunk = keep + moved(give, "col", swap)
    up = chunk[4]
    down = chunk[5]
    for s, t in ((3, 6), (2, 7), (1, 0)):
        up, down = together(moved(up, "col", ahead_one), moved(down, "col", behind_one))
        if s == 3:
            up, down, corner_front = together(up, down, corner_front)
        if s == 1:
            up, down, raw = together(up, down, moved(raw, "front", next_front))
        up = chunk[s] + up
        down = chunk[t] + down
    corner = corner_front + moved(down[:1], both_axes, hop) + moved(up[:1], both_axes, hop_ahead)

    quad = jnp.concatenate(
        [corner] + [moved(corner, "row", [(i, (i + s) % ROWS) for i in range(ROWS)]) for s in (1, 2, 3)], 0
    )

    body_front = after(stored[0, 2:], down)
    body_front = jnp.where(h == 0, moved(body_front[:3], "col", to_even), moved(body_front[3:], "col", to_odd))
    quad, body_front = together(quad, body_front)
    up, down = after([up, down], quad)
    body = body_front + moved(down[1:], both_axes, hop) + moved(up[1:], both_axes, hop_ahead)
    half_rows = ((2 + 3 * h + jnp.arange(3)) * ROWS + r)[:, None, None]
    body = jnp.where(half_rows * T + jnp.arange(T)[:, None] < limit, body, 0.0)
    gathered = lax.all_gather(body, "col", axis=0, tiled=False).reshape(NB, 6, T, T)

    pieces = {0: quad}
    ahead = behind = quad
    for s in (1, 2, 3):
        ahead, behind = together(moved(ahead, "col", ahead_one), moved(behind, "col", behind_one))
        pieces[s] = ahead
        pieces[NB - s] = behind
    own = jnp.stack([pieces[s] for s in sorted(pieces)])
    far, other = together(moved(behind, "col", behind_one), moved(own, "col", swap))
    other_far = moved(far, "col", swap)

    raw = after(raw, quad)
    send = slot_call(raw[:, T, 0].astype(jnp.int32), raw)
    arrived = lax.all_to_all(after(send, far), "col", split_axis=0, concat_axis=0, tiled=True)
    part0 = corner_call(0, after(ids, body), own, other, far, other_far)

    first_done = part0[1]

    gathered = after(gathered, first_done)
    pick = [jnp.maximum(c // ROWS - 2, 0), c // ROWS + 2]
    chosen = jnp.concatenate([lax.dynamic_slice_in_dim(gathered, p, 1, axis=1) for p in pick], 1)
    sent = [chosen]
    for s in (1, 2, 3):
        pairs = [(i % ROWS * COLS + i, (i % ROWS + s) % ROWS * COLS + i) for i in range(COLS)]
        sent.append(moved(chosen, ("row", "col"), pairs))
    part1 = corner_call(1, after(ids, chosen), part0[2], part0[0], part0[1], gathered.reshape(NB, 6 * T, T))
    part2 = corner_call(2, ids, part1[2], part1[0], part1[1], part1[-1])
    parts = (part0, part1, part2)

    arrived = after(arrived, part1[1])
    marks = arrived[:, T, 0].astype(jnp.int32)
    result = last_call(ids, marks, parts, sent, stored, arrived)
    return result.reshape(front.shape)


def solution(mesh):
    spec = P("front", None, "row", None, None, "col", None)
    placed = (
        spec,
        P("front", ("row", "col"), None, None),
        P("front", ("row", "col"), None),
        P("front", ("row", "col")),
        P("front", ("row", "col")),
        P("front"),
    )
    return jax.shard_map(on_device, mesh=mesh, in_specs=placed, out_specs=spec, check_vma=False)
```

```python
import jax
import jax.numpy as jnp
from jax import lax
from jax.experimental import pallas as pl
from jax.experimental.pallas import tpu as pltpu
from jax.sharding import PartitionSpec as P

T = 128
G = 8
NB = 8
ROWS = 4
COLS = 16
VMEM_LIMIT = 60 * 1024 * 1024


def params():
    return pltpu.CompilerParams(vmem_limit_bytes=VMEM_LIMIT)


def split(x):
    h = x.astype(jnp.bfloat16)
    x = x - h.astype(jnp.float32)
    m = x.astype(jnp.bfloat16)
    low = (x - m.astype(jnp.float32)).astype(jnp.bfloat16)
    return h, m, low


def left_terms(x, axis):
    h, m, low = split(x)
    return jnp.concatenate([h, h, m, h, low, m], axis)


def right_terms(x, axis):
    h, m, low = split(x)
    return jnp.concatenate([h, m, h, low, h, m], axis)


def short_left(x):
    h, m, low = split(x)
    return jnp.concatenate([h, h, m], 1)


def short_right(x):
    h, m, low = split(x)
    return jnp.concatenate([h, m, h], 1)


def dot_rows(a, b):
    return lax.dot_general(a, b, (((1,), (1,)), ((), ())), preferred_element_type=jnp.float32)


def dot_columns(a, b):
    return lax.dot_general(a, b, (((0,), (0,)), ((), ())), preferred_element_type=jnp.float32)


def factor_tile(s_ref, w_ref, spare):
    span = 32
    rows = lax.broadcasted_iota(jnp.int32, (T, T), 0)
    lanes = lax.broadcasted_iota(jnp.int32, (T, T), 1)
    w_ref[...] = (rows == lanes).astype(jnp.float32)
    sub = lax.broadcasted_iota(jnp.int32, (G, T), 0)
    lane = lax.broadcasted_iota(jnp.int32, (G, T), 1)
    count = span // G
    done = 0
    for base in range(0, T, span):
        left = [s_ref[base + G * g:base + G * (g + 1), :] for g in range(count)]
        right = [w_ref[base + G * g:base + G * (g + 1), :] for g in range(count)]
        for g in range(count):
            r0 = base + G * g
            R, W = left[g], right[g]
            e = [[None] * G for _ in range(G)]
            for t in range(G):
                column = jnp.broadcast_to(R[:, r0 + t:r0 + t + 1], (G, T))
                for s in range(t + 1):
                    e[s][t] = jnp.broadcast_to(column[s:s + 1, :], (G, T))
            a = [jnp.broadcast_to(R[t:t + 1, :], (G, T)) for t in range(G)]
            w = [jnp.broadcast_to(W[t:t + 1, :], (G, T)) for t in range(G)]
            c = {
                i: [jnp.broadcast_to(left[i][:, r0 + t:r0 + t + 1], (G, T)) for t in range(G)]
                for i in range(g + 1, count)
            }
            U = jnp.zeros((G, T), jnp.float32)
            X = jnp.zeros((G, T), jnp.float32)
            for t in range(G):
                rec = 1.0 / e[t][t]
                root = lax.rsqrt(e[t][t])
                m = {}
                for s in range(t + 1, G):
                    m[s] = e[t][s] * rec
                    for q in range(s, G):
                        if s == t + 1 and q == s:
                            e[s][q] = e[s][q] - (e[t][s] * e[t][q]) * rec
                        else:
                            e[s][q] = e[s][q] - m[s] * e[t][q]
                for s in range(t + 1, G):
                    a[s] = a[s] - m[s] * a[t]
                    w[s] = w[s] - m[s] * w[t]
                U = jnp.where(sub == t, a[t] * root, U)
                X = jnp.where(sub == t, w[t] * root, X)
                for i in range(g + 1, count):
                    for s in range(t + 1, G):
                        c[i][s] = c[i][s] - m[s] * c[i][t]
                    ct = c[i][t] * rec
                    left[i] = left[i] - ct * a[t]
                    right[i] = right[i] - ct * w[t]
            left[g] = jnp.where(lane >= r0 + sub, U, 0.0)
            right[g] = X
            step = (base + G * g) // G + 1
            while done * (T // G) < len(spare) * step:
                spare[done]()
                done += 1
        U = jnp.concatenate(left, 0)
        X = jnp.concatenate(right, 0)
        s_ref[base:base + span, :] = U
        w_ref[base:base + span, :] = X
        end = base + span
        if end < T:
            prod = dot_columns(left_terms(U, 0), right_terms(jnp.concatenate([U, X], 1), 0))
            s_ref[end:, :] = s_ref[end:, :] - prod[end:, :T]
            w_ref[end:, :] = w_ref[end:, :] - prod[end:, T:]


CUTS = (0, 3, 6, 8)
PARTS = len(CUTS) - 1


def home(j):
    return j // 2 if j % 2 == 0 else NB - 1 - j // 2


def row_work(before, first, done_ref, w_ref, x_ref, parts_ref, left_ref, terms_ref, solved_ref):
    seen = set()

    def get(j):
        if j not in seen:
            return x_ref[home(j)] if before == 0 else x_ref[j - before]
        return solved_ref[j - before] if j < first else left_ref[j - first]

    def put(j, value):
        seen.add(j)
        if j < first:
            solved_ref[j - before] = value
        else:
            left_ref[j - first] = value

    def solve(k):
        x = dot_rows(short_left(get(k)), short_right(w_ref[k - before]))
        put(k, x)
        terms_ref[:, 3 * T * (k - before):3 * T * (k - before + 1)] = short_left(x)
        parts_ref[:, 2 * T * (k - before):2 * T * (k - before + 1)] = short_left(x)[:, T:]

    def update(k, j, hi):
        terms = terms_ref[:, 3 * T * (k - before):3 * T * (k - before + 1)]
        d = dot_rows(terms, short_right(done_ref[k - before, (j - before) * T:(hi - before) * T, :]))
        for i in range(j, hi):
            put(i, get(i) - d[:, (i - j) * T:(i - j + 1) * T])

    work = []
    for k in range(before, first):
        work.append(lambda k=k: solve(k))
        for j in range(k + 1, NB, 2):
            work.append(lambda k=k, j=j: update(k, j, min(j + 2, NB)))
    return work


def fetch(source, target, sem):
    copy = pltpu.make_async_copy(source, target, sem)
    copy.start()
    return copy


def corner_part(first, last, refs):
    ids_ref = refs[0]
    others = []
    inputs = 4
    ins, refs = refs[1:1 + inputs], refs[1 + inputs:]
    count = 2 + (last < NB) + 3 * (first > 0)
    outs, refs = refs[:count], refs[count:]
    held, refs = refs[:count], refs[count:]
    done_ref, w_ref = held[:2]
    rest_ref = held[2] if last < NB else None
    s_ref, xl_ref, xr_ref, in_sems, out_sems = refs[:5]
    refs = refs[5:]
    sent = []

    def store(source, target):
        sent.append(fetch(source, target, out_sems.at[len(sent)]))

    def put(j, lo, hi, value):
        if j < last:
            done_ref[j - first, (lo - first) * T:(hi - first) * T, :] = value
        else:
            rest_ref[j - last, (lo - last) * T:(hi - last) * T, :] = value

    def get(j, lo, hi):
        if j < last:
            return done_ref[j - first, (lo - first) * T:(hi - first) * T, :]
        return rest_ref[j - last, (lo - last) * T:(hi - last) * T, :]

    rows = lax.broadcasted_iota(jnp.int32, (T, T), 0)
    lanes = lax.broadcasted_iota(jnp.int32, (T, T), 1)
    if first == 0:
        own_ref, other_ref, own_far_ref, other_far_ref = refs
        z = ids_ref[0]
        h = ids_ref[1]
        r = ids_ref[2]
        copies = [fetch(ins[n], refs[n], in_sems.at[n]) for n in range(inputs)]
        for copy in copies:
            copy.wait()

        def assemble(j, lo, hi):
            s = (z + NB - home(j)) % NB
            for i in range(lo, hi):
                t = (r + NB - i) % ROWS
                near = jnp.where(s > 4, s - 1, jnp.minimum(s, 3))
                value = jnp.where(
                    s == 4,
                    jnp.where(h == i // ROWS, own_far_ref[t], other_far_ref[t]),
                    jnp.where(h == i // ROWS, own_ref[near, t], other_ref[near, t]),
                )
                if i == j:
                    low = jnp.where(rows >= lanes, value, 0.0)
                    value = low + jnp.where(rows > lanes, value, 0.0).T
                put(j, i, i + 1, value)

        assemble(0, 0, 1)
        s_ref[...] = get(0, 0, 1)
        spare = [lambda: assemble(0, 1, NB)] + [lambda j=j: assemble(j, j, NB) for j in range(1, NB)]
    else:
        before = CUTS[CUTS.index(first) - 1]
        state_ref, old_ref, old_w_ref, x_ref, terms_ref, solved_ref, tile_ref, last_ref = refs
        parts_ref, column_ref, left_ref = held[-3:]
        width = first - before
        early = [
            fetch(ins[0].at[0, pl.ds(0, T)], tile_ref, in_sems.at[4]),
            fetch(ins[1].at[width - 1, pl.ds(width * T, (NB - first) * T)], last_ref, in_sems.at[5]),
        ]
        late = [fetch(ins[n], ref, in_sems.at[n]) for n, ref in enumerate((state_ref, old_ref, old_w_ref, x_ref))]
        for copy in early:
            copy.wait()
        xl_ref[first * T:(first + 1) * T, :] = left_terms(last_ref[:T, :], 1)
        xr_ref[first * T:(first + 1) * T, :] = right_terms(last_ref[:T, :], 1)
        s_ref[...] = tile_ref[...] - dot_rows(xl_ref[first * T:(first + 1) * T, :], xr_ref[first * T:(first + 1) * T, :])

        def take():
            late[0].wait()
            put(first, first + 1, NB, state_ref[0, T:, :])
            for j in range(first + 1, NB):
                put(j, j, NB, state_ref[j - first, (j - first) * T:, :])

        def last_terms():
            xl_ref[(first + 1) * T:, :] = left_terms(last_ref[T:, :], 1)
            xr_ref[(first + 1) * T:, :] = right_terms(last_ref[T:, :], 1)

        def arrive():
            for copy in late[1:]:
                copy.wait()

        spare = [take, last_terms, lambda: trail(first, first + 1)]
        for j in range(first + 1, NB, 2):
            spare.append((lambda j=j: trail_pair(j)) if j + 1 < NB else (lambda j=j: trail(j, j)))
        others = [arrive] + row_work(before, first, old_ref, old_w_ref, x_ref, parts_ref, left_ref, terms_ref, solved_ref)
    for j in range(first + 1, last):
        done_ref[j - first, :(j - first) * T, :] = jnp.zeros(((j - first) * T, T), jnp.float32)

    def panel(k, lo, hi):
        x = dot_rows(left_terms(get(k, lo, hi), 1), right_terms(w_ref[k - first], 1))
        put(k, lo, hi, x)
        xl_ref[lo * T:hi * T, :] = left_terms(x, 1)
        xr_ref[lo * T:hi * T, :] = right_terms(x, 1)

    def trail(j, lo):
        put(j, lo, NB, get(j, lo, NB) - dot_rows(xl_ref[lo * T:, :], xr_ref[j * T:(j + 1) * T, :]))

    def trail_pair(j):
        d = dot_rows(xl_ref[j * T:, :], xr_ref[j * T:(j + 2) * T, :])
        put(j, j, NB, get(j, j, NB) - d[:, :T])
        put(j + 1, j + 1, NB, get(j + 1, j + 1, NB) - d[T:, T:])

    for k in range(first, last):
        share = -(-len(others) // (last - k))
        spare, others = spare + others[:share], others[share:]
        factor_tile(s_ref, w_ref.at[k - first], spare)
        put(k, k, k + 1, s_ref[...].T)
        if k > first:
            store(done_ref.at[k - 1 - first], outs[0].at[k - 1 - first])
        n = k + 1
        if n == last:
            if first > 0:
                column_ref[...] = solved_ref[jnp.clip(ids_ref[3] - before, 0, first - before - 1)]
            for i in range(1, count):
                store(held[i], outs[i])
            if n < NB:
                panel(k, n, NB)
            break
        panel(k, n, n + 1)
        s_ref[...] = get(n, n, n + 1) - dot_rows(xl_ref[n * T:(n + 1) * T, :], xr_ref[n * T:(n + 1) * T, :])
        spare = []
        if n + 1 < NB:
            spare.append(lambda k=k, n=n: panel(k, n + 1, NB))
            spare.append(lambda n=n: trail(n, n + 1))
            for j in range(n + 1, NB, 2):
                if j + 1 < NB:
                    spare.append(lambda j=j: trail_pair(j))
                else:
                    spare.append(lambda j=j: trail(j, j))
    store(done_ref.at[last - 1 - first], outs[0].at[last - 1 - first])
    for copy in sent:
        copy.wait()


def corner_call(part, ids, *state):
    first, last = CUTS[part], CUTS[part + 1]
    smem = pl.BlockSpec(memory_space=pltpu.SMEM)
    far = pl.BlockSpec(memory_space=pl.ANY)
    span = (NB - first) * T
    shapes = [((last - first, span, T), jnp.float32), ((last - first, T, T), jnp.float32)]
    if last < NB:
        shapes.append(((NB - last, (NB - last) * T, T), jnp.float32))
    extra = [pltpu.VMEM(x.shape, x.dtype) for x in state]
    if first > 0:
        width = first - CUTS[part - 1]
        shapes.append(((6 * T, 2 * T * width), jnp.bfloat16))
        shapes.append(((6 * T, T), jnp.float32))
        shapes.append(((NB - first, 6 * T, T), jnp.float32))
        extra += [pltpu.VMEM((6 * T, 3 * T * width), jnp.bfloat16), pltpu.VMEM((width, 6 * T, T), jnp.float32)]
        extra += [pltpu.VMEM((T, T), jnp.float32), pltpu.VMEM((span, T), jnp.float32)]

    def kernel(*refs):
        corner_part(first, last, refs)

    return pl.pallas_call(
        kernel,
        in_specs=[smem] + [far] * len(state),
        out_specs=[far] * len(shapes),
        out_shape=[jax.ShapeDtypeStruct(*x) for x in shapes],
        scratch_shapes=[pltpu.VMEM(*x) for x in shapes]
        + [
            pltpu.VMEM((T, T), jnp.float32),
            pltpu.VMEM((NB * T, 6 * T), jnp.bfloat16),
            pltpu.VMEM((NB * T, 6 * T), jnp.bfloat16),
            pltpu.SemaphoreType.DMA((len(state) + 2,)),
            pltpu.SemaphoreType.DMA((last - first + len(shapes) - 1,)),
            *extra,
        ],
        compiler_params=params(),
    )(ids, *state)


def last_kernel(*refs):
    ids_ref, mark_ref = refs[:2]
    count = 3 * PARTS + 2
    ins, refs = refs[2:2 + count], refs[2 + count:]
    sent_in, refs = refs[:4], refs[4:]
    column_in, refs = refs[:PARTS - 1], refs[PARTS - 1:]
    out_ref = refs[0]
    held, refs = refs[1:1 + count], refs[1 + count:]
    done_refs, w_refs, parts_refs = held[:PARTS], held[PARTS:2 * PARTS], held[2 * PARTS:3 * PARTS - 1]
    left_ref, front_ref, tiles_ref = held[3 * PARTS - 1:]
    sent_ref, column_ref, x_ref, xa_ref, xb_ref, pad_ref, sems = refs
    behind = CUTS[-2]
    r = ids_ref[2]
    c = ids_ref[3]
    which = (r + ROWS - c % ROWS) % ROWS
    for s, ref in enumerate(sent_in):
        @pl.when(which == s)
        def _(ref=ref):
            fetch(ref, sent_ref, sems.at[count])

    copies = [None] * count
    order = [n for part in range(PARTS) for n in (part, PARTS + part)] + [3 * PARTS - 1]
    for n in order + [n for n in range(count) if n not in order]:
        copies[n] = fetch(ins[n], held[n], sems.at[n])
    pltpu.make_async_copy(sent_in[0], sent_ref, sems.at[count]).wait()
    for k in range(NB):
        x_ref[k, :2 * T] = sent_ref[home(k)].reshape(2 * T, T)

    rows = 8 * T
    for k in range(NB):
        part = sum(k >= cut for cut in CUTS[1:-1])
        first = CUTS[part]
        done_ref, w_ref = done_refs[part], w_refs[part]
        if k == first:
            copies[part].wait()
            copies[PARTS + part].wait()
        if k == behind:
            copies[3 * PARTS - 1].wait()
            for j in range(behind, NB):
                x_ref[j, 2 * T:] = left_ref[j - behind]
        high = rows if k >= behind else 2 * T
        x = dot_rows(short_left(x_ref[k, :high]), short_right(w_ref[k - first]))
        x_ref[k, :high] = x
        xb_ref[:, 3 * T * k:3 * T * (k + 1)] = short_right(x[:2 * T])
        terms = short_left(x)
        if k >= behind:
            xa_ref[:, 3 * T * (k - behind):3 * T * (k - behind + 1)] = terms[2 * T:]
        for j in range(k + 1, NB, 2):
            hi = min(j + 2, NB)
            d = dot_rows(terms, short_right(done_ref[k - first, (j - first) * T:(hi - first) * T, :]))
            for i in range(j, hi):
                x_ref[i, :high] = x_ref[i, :high] - d[:, (i - j) * T:(i - j + 1) * T]
    for copy in copies[2 * PARTS:3 * PARTS - 1] + copies[3 * PARTS:]:
        copy.wait()
    for b in range(2):
        pad_ref[b] = front_ref[b, 2:]

    def add_tile(s, carry):
        mark = mark_ref[s] - 1

        @pl.when(mark >= 0)
        def _():
            b = mark // 8
            a = mark % 8 - 2
            pad_ref[b, a] = pad_ref[b, a] + tiles_ref[s, :T, :]

        return carry

    lax.fori_loop(0, 2 * COLS, add_tile, 0)
    pieces = []
    for n, ref in enumerate(parts_refs):
        for k in range(CUTS[n + 1] - CUTS[n]):
            h = ref[:, 2 * T * k:2 * T * k + T]
            pieces += [h, ref[:, 2 * T * k:2 * T * (k + 1)]]
    product = dot_rows(jnp.concatenate(pieces + [xa_ref[...]], 1), xb_ref[...])
    limit = ids_ref[4]
    lower = lax.broadcasted_iota(jnp.int32, (T, T), 0)
    lanes = lax.broadcasted_iota(jnp.int32, (T, T), 1)

    def padded(b):
        j = (b * COLS + c) * T + lanes
        tiles = []
        for a in range(6):
            i = ((a + 2) * ROWS + r) * T + lower
            unit = jnp.where(i == j, 1.0, 0.0)
            tiles.append(jnp.where(jnp.logical_and(i < limit, j < limit), pad_ref[b, a], unit))
        return jnp.concatenate(tiles, 0)

    in_panel = c < NB
    zeros = jnp.zeros((2 * T, T), jnp.float32)
    out_ref[pl.Slice(0, 2 * T, 2), :] = zeros
    out_ref[pl.Slice(1, 2 * T, 2), :] = zeros
    out_ref[pl.Slice(4 * T + 1, 6 * T, 2), :] = padded(1) - product[:, T:]

    @pl.when(jnp.logical_not(in_panel))
    def _():
        out_ref[pl.Slice(4 * T, 6 * T, 2), :] = padded(0) - product[:, :T]

    for n, ref in enumerate(column_in):
        @pl.when(jnp.logical_and(c >= CUTS[n], c < CUTS[n + 1]))
        def _(n=n, ref=ref):
            copy = fetch(ref, column_ref, sems.at[count + 1])
            copy.wait()
            out_ref[pl.Slice(4 * T, 6 * T, 2), :] = column_ref[...]

    @pl.when(jnp.logical_and(c >= behind, c < NB))
    def _():
        out_ref[pl.Slice(4 * T, 6 * T, 2), :] = x_ref[jnp.clip(c, behind, NB - 1), 2 * T:]

    for a in range(2):
        i = r + ROWS * a
        for part, ref in enumerate(done_refs):
            first, last = CUTS[part], CUTS[part + 1]

            @pl.when(jnp.logical_and(jnp.logical_and(c >= first, c < last), i >= first))
            def _(ref=ref, first=first, last=last, a=a):
                at = pl.multiple_of(jnp.maximum(i - first, 0) * T, T)
                out_ref[pl.Slice(2 * a * T, T, 2), :] = ref[jnp.clip(c - first, 0, last - first - 1), pl.ds(at, T), :]


def last_call(ids, marks, parts, sent, front, tiles):
    smem = pl.BlockSpec(memory_space=pltpu.SMEM)
    vmem = pl.BlockSpec(memory_space=pltpu.VMEM)
    far = pl.BlockSpec(memory_space=pl.ANY)
    operands = [p[0] for p in parts] + [p[1] for p in parts]
    operands += [p[-3] for p in parts[1:]] + [parts[-1][-1], front, tiles]
    others = list(sent) + [p[-2] for p in parts[1:]]
    return pl.pallas_call(
        last_kernel,
        in_specs=[smem, smem] + [far] * (len(operands) + len(others)),
        out_specs=vmem,
        out_shape=jax.ShapeDtypeStruct((16 * T, T), jnp.float32),
        scratch_shapes=[pltpu.VMEM(x.shape, x.dtype) for x in operands]
        + [
            pltpu.VMEM((NB, 2, T, T), jnp.float32),
            pltpu.VMEM((6 * T, T), jnp.float32),
            pltpu.VMEM((NB, NB * T, T), jnp.float32),
            pltpu.VMEM((6 * T, 3 * T * (NB - CUTS[-2])), jnp.bfloat16),
            pltpu.VMEM((2 * T, 3 * T * NB), jnp.bfloat16),
            pltpu.VMEM((2, 6, T, T), jnp.float32),
            pltpu.SemaphoreType.DMA((len(operands) + 2,)),
        ],
        compiler_params=params(),
    )(ids, marks, *operands, *others)


def scatter_kernel(ids_ref, owner_ref, row_ref, col_ref, tiles_ref, keep_ref, give_ref, raw_ref):
    z = ids_ref[0]
    h = ids_ref[1]
    keep_ref[...] = jnp.zeros(keep_ref.shape, jnp.float32)
    give_ref[...] = jnp.zeros(give_ref.shape, jnp.float32)

    def step(i, carry):
        o = owner_ref[i]
        a = row_ref[i]
        b = col_ref[i]
        panel = jnp.logical_and(b == 0, o < NB)

        @pl.when(panel)
        def _():
            core = jnp.where(a < 2, a, (a - 2) // 3)
            place = jnp.where(a < 2, 0, a - 1 - 3 * core)
            p = (jnp.where(o % 2 == 0, o // 2, NB - 1 - o // 2) + NB - z) % NB

            @pl.when(core == h)
            def _():
                keep_ref[p, place] = keep_ref[p, place] + tiles_ref[i]

            @pl.when(core != h)
            def _():
                give_ref[p, place] = give_ref[p, place] + tiles_ref[i]

        mark = jnp.where(jnp.logical_or(panel, a < 2), 0, o * 16 + b * 8 + a + 1)
        raw_ref[i, :T, :] = tiles_ref[i]
        raw_ref[i, T:, :] = jnp.full((8, T), mark.astype(jnp.float32), jnp.float32)
        return carry

    lax.fori_loop(0, owner_ref.shape[0], step, 0)


def scatter_call(ids, owner, row, col, tiles):
    smem = pl.BlockSpec(memory_space=pltpu.SMEM)
    vmem = pl.BlockSpec(memory_space=pltpu.VMEM)
    return pl.pallas_call(
        scatter_kernel,
        in_specs=[smem, smem, smem, smem, vmem],
        out_specs=[vmem, vmem, vmem],
        out_shape=[
            jax.ShapeDtypeStruct((NB, 4, T, T), jnp.float32),
            jax.ShapeDtypeStruct((NB, 4, T, T), jnp.float32),
            jax.ShapeDtypeStruct((COLS, T + 8, T), jnp.float32),
        ],
        compiler_params=params(),
    )(ids, owner, row, col, tiles)


def slot_kernel(mark_ref, raw_ref, send_ref, count_ref):
    for o in range(COLS):
        send_ref[2 * o, T:, :] = jnp.zeros((8, T), jnp.float32)
        send_ref[2 * o + 1, T:, :] = jnp.zeros((8, T), jnp.float32)
        count_ref[o] = 0

    def step(i, carry):
        mark = mark_ref[i] - 1

        @pl.when(mark >= 0)
        def _():
            o = mark // 16
            slot = 2 * o + count_ref[o]
            count_ref[o] = count_ref[o] + 1
            send_ref[slot, :T, :] = raw_ref[i, :T, :]
            send_ref[slot, T:, :] = jnp.full((8, T), (mark % 16 + 1).astype(jnp.float32), jnp.float32)

        return carry

    lax.fori_loop(0, COLS, step, 0)


def slot_call(marks, raw):
    smem = pl.BlockSpec(memory_space=pltpu.SMEM)
    vmem = pl.BlockSpec(memory_space=pltpu.VMEM)
    return pl.pallas_call(
        slot_kernel,
        in_specs=[smem, vmem],
        out_specs=vmem,
        out_shape=jax.ShapeDtypeStruct((2 * COLS, T + 8, T), jnp.float32),
        scratch_shapes=[pltpu.SMEM((COLS,), jnp.int32)],
        compiler_params=params(),
    )(marks, raw)


def moved(value, axes, pairs):
    return lax.ppermute(value, axes, pairs)


def together(*values):
    return lax.optimization_barrier(values)


def after(value, *others):
    return lax.optimization_barrier((value, *others))[0]


def on_device(front, child_tiles, child_owner, child_row, child_col, front_size):
    r = lax.axis_index("row")
    c = lax.axis_index("col")
    z = c // 2
    h = c % 2
    limit = front_size[0]
    stored = front.reshape(8, T, 2, T).transpose(2, 0, 1, 3)
    ids = jnp.stack([z, h, r, c, limit]).astype(jnp.int32)
    next_front = [(f, (f + 1) % 4) for f in range(4)]
    ahead_one = [(i, (i + 2) % COLS) for i in range(COLS)]
    behind_one = [(i, (i - 2) % COLS) for i in range(COLS)]
    swap = [(i, i ^ 1) for i in range(COLS)]
    both_axes = ("front", "col")
    hop = [(f * COLS + i, (f + 1) % 4 * COLS + i) for f in range(4) for i in range(COLS)]
    hop_ahead = [(f * COLS + i, (f + 1) % 4 * COLS + (i + 2) % COLS) for f in range(4) for i in range(COLS)]

    keep, give, raw = scatter_call(ids, child_owner[0, :, 0], child_row[0], child_col[0], child_tiles[0])

    to_even = [(j, 2 * home(j)) for j in range(NB)]
    to_odd = [(j, 2 * home(j) + 1) for j in range(NB)]
    corner_front = jnp.where(h == 0, moved(stored[0, :1], "col", to_even), moved(stored[0, 1:2], "col", to_odd))

    chunk = keep + moved(give, "col", swap)
    up = chunk[4]
    down = chunk[5]
    for s, t in ((3, 6), (2, 7), (1, 0)):
        up, down = together(moved(up, "col", ahead_one), moved(down, "col", behind_one))
        if s == 3:
            up, down, corner_front = together(up, down, corner_front)
        if s == 1:
            up, down, raw = together(up, down, moved(raw, "front", next_front))
        up = chunk[s] + up
        down = chunk[t] + down
    corner = corner_front + moved(down[:1], both_axes, hop) + moved(up[:1], both_axes, hop_ahead)

    quad = jnp.concatenate(
        [corner] + [moved(corner, "row", [(i, (i + s) % ROWS) for i in range(ROWS)]) for s in (1, 2, 3)], 0
    )

    body_front = after(stored[0, 2:], down)
    body_front = jnp.where(h == 0, moved(body_front[:3], "col", to_even), moved(body_front[3:], "col", to_odd))
    quad, body_front = together(quad, body_front)
    up, down = after([up, down], quad)
    body = body_front + moved(down[1:], both_axes, hop) + moved(up[1:], both_axes, hop_ahead)
    half_rows = ((2 + 3 * h + jnp.arange(3)) * ROWS + r)[:, None, None]
    body = jnp.where(half_rows * T + jnp.arange(T)[:, None] < limit, body, 0.0)
    gathered = lax.all_gather(body, "col", axis=0, tiled=False).reshape(NB, 6, T, T)

    pieces = {0: quad}
    ahead = behind = quad
    for s in (1, 2, 3):
        ahead, behind = together(moved(ahead, "col", ahead_one), moved(behind, "col", behind_one))
        pieces[s] = ahead
        pieces[NB - s] = behind
    own = jnp.stack([pieces[s] for s in sorted(pieces)])
    far, other = together(moved(behind, "col", behind_one), moved(own, "col", swap))
    other_far = moved(far, "col", swap)

    raw = after(raw, quad)
    send = slot_call(raw[:, T, 0].astype(jnp.int32), raw)
    arrived = lax.all_to_all(after(send, far), "col", split_axis=0, concat_axis=0, tiled=True)
    part0 = corner_call(0, after(ids, body), own, other, far, other_far)

    first_done = part0[1]

    gathered = after(gathered, first_done)
    pick = [jnp.maximum(c // ROWS - 2, 0), c // ROWS + 2]
    chosen = jnp.concatenate([lax.dynamic_slice_in_dim(gathered, p, 1, axis=1) for p in pick], 1)
    sent = [chosen]
    for s in (1, 2, 3):
        pairs = [(i % ROWS * COLS + i, (i % ROWS + s) % ROWS * COLS + i) for i in range(COLS)]
        sent.append(moved(chosen, ("row", "col"), pairs))
    parts = [part0, corner_call(1, after(ids, chosen), part0[2], part0[0], part0[1], gathered.reshape(NB, 6 * T, T))]
    arrived = after(arrived, parts[1][1])
    for part in range(2, PARTS):
        old = parts[-1]
        parts.append(corner_call(part, ids, old[2], old[0], old[1], old[-1]))
    marks = arrived[:, T, 0].astype(jnp.int32)
    result = last_call(ids, marks, parts, sent, stored, arrived)
    return result.reshape(front.shape)


def solution(mesh):
    spec = P("front", None, "row", None, None, "col", None)
    placed = (
        spec,
        P("front", ("row", "col"), None, None),
        P("front", ("row", "col"), None),
        P("front", ("row", "col")),
        P("front", ("row", "col")),
        P("front"),
    )
    return jax.shard_map(on_device, mesh=mesh, in_specs=placed, out_specs=spec, check_vma=False)
```

```python
import jax
import jax.numpy as jnp
from jax import lax
from jax.experimental import pallas as pl
from jax.experimental.pallas import tpu as pltpu
from jax.sharding import PartitionSpec as P

T = 128
G = 8
NB = 8
ROWS = 4
COLS = 16
VMEM_LIMIT = 60 * 1024 * 1024


def params(limit=VMEM_LIMIT):
    return pltpu.CompilerParams(vmem_limit_bytes=limit)


def split(x):
    h = x.astype(jnp.bfloat16)
    x = x - h.astype(jnp.float32)
    m = x.astype(jnp.bfloat16)
    low = (x - m.astype(jnp.float32)).astype(jnp.bfloat16)
    return h, m, low


def left_terms(x, axis):
    h, m, low = split(x)
    return jnp.concatenate([h, h, m, h, low, m], axis)


def right_terms(x, axis):
    h, m, low = split(x)
    return jnp.concatenate([h, m, h, low, h, m], axis)


def short_left(x):
    h, m, low = split(x)
    return jnp.concatenate([h, h, m], 1)


def short_right(x):
    h, m, low = split(x)
    return jnp.concatenate([h, m, h], 1)


def dot_rows(a, b):
    return lax.dot_general(a, b, (((1,), (1,)), ((), ())), preferred_element_type=jnp.float32)


def dot_columns(a, b):
    return lax.dot_general(a, b, (((0,), (0,)), ((), ())), preferred_element_type=jnp.float32)


def factor_tile(s_ref, w_ref, spare):
    span = 32
    rows = lax.broadcasted_iota(jnp.int32, (T, T), 0)
    lanes = lax.broadcasted_iota(jnp.int32, (T, T), 1)
    w_ref[...] = (rows == lanes).astype(jnp.float32)
    sub = lax.broadcasted_iota(jnp.int32, (G, T), 0)
    lane = lax.broadcasted_iota(jnp.int32, (G, T), 1)
    count = span // G
    done = 0
    for base in range(0, T, span):
        left = [s_ref[base + G * g:base + G * (g + 1), :] for g in range(count)]
        right = [w_ref[base + G * g:base + G * (g + 1), :] for g in range(count)]
        for g in range(count):
            r0 = base + G * g
            R, W = left[g], right[g]
            e = [[None] * G for _ in range(G)]
            for t in range(G):
                column = jnp.broadcast_to(R[:, r0 + t:r0 + t + 1], (G, T))
                for s in range(t + 1):
                    e[s][t] = jnp.broadcast_to(column[s:s + 1, :], (G, T))
            a = [jnp.broadcast_to(R[t:t + 1, :], (G, T)) for t in range(G)]
            w = [jnp.broadcast_to(W[t:t + 1, :], (G, T)) for t in range(G)]
            c = {
                i: [jnp.broadcast_to(left[i][:, r0 + t:r0 + t + 1], (G, T)) for t in range(G)]
                for i in range(g + 1, count)
            }
            U = jnp.zeros((G, T), jnp.float32)
            X = jnp.zeros((G, T), jnp.float32)
            for t in range(G):
                rec = 1.0 / e[t][t]
                root = lax.rsqrt(e[t][t])
                m = {}
                for s in range(t + 1, G):
                    m[s] = e[t][s] * rec
                    for q in range(s, G):
                        if s == t + 1 and q == s:
                            e[s][q] = e[s][q] - (e[t][s] * e[t][q]) * rec
                        else:
                            e[s][q] = e[s][q] - m[s] * e[t][q]
                for s in range(t + 1, G):
                    a[s] = a[s] - m[s] * a[t]
                    w[s] = w[s] - m[s] * w[t]
                U = jnp.where(sub == t, a[t] * root, U)
                X = jnp.where(sub == t, w[t] * root, X)
                for i in range(g + 1, count):
                    for s in range(t + 1, G):
                        c[i][s] = c[i][s] - m[s] * c[i][t]
                    ct = c[i][t] * rec
                    left[i] = left[i] - ct * a[t]
                    right[i] = right[i] - ct * w[t]
            left[g] = jnp.where(lane >= r0 + sub, U, 0.0)
            right[g] = X
            step = (base + G * g) // G + 1
            while done * (T // G) < len(spare) * step:
                spare[done]()
                done += 1
        U = jnp.concatenate(left, 0)
        X = jnp.concatenate(right, 0)
        s_ref[base:base + span, :] = U
        w_ref[base:base + span, :] = X
        end = base + span
        if end < T:
            prod = dot_columns(left_terms(U, 0), right_terms(jnp.concatenate([U, X], 1), 0))
            s_ref[end:, :] = s_ref[end:, :] - prod[end:, :T]
            w_ref[end:, :] = w_ref[end:, :] - prod[end:, T:]


CUTS = (0, 3, 6, 8)
PARTS = len(CUTS) - 1


def home(j):
    return j // 2 if j % 2 == 0 else NB - 1 - j // 2


def row_work(before, first, done_ref, w_ref, x_ref, parts_ref, left_ref, terms_ref, solved_ref):
    seen = set()

    def get(j):
        if j not in seen:
            return x_ref[home(j)] if before == 0 else x_ref[j - before]
        return solved_ref[j - before] if j < first else left_ref[j - first]

    def put(j, value):
        seen.add(j)
        if j < first:
            solved_ref[j - before] = value
        else:
            left_ref[j - first] = value

    def solve(k):
        x = dot_rows(short_left(get(k)), short_right(w_ref[k - before]))
        put(k, x)
        terms_ref[:, 3 * T * (k - before):3 * T * (k - before + 1)] = short_left(x)
        parts_ref[:, 2 * T * (k - before):2 * T * (k - before + 1)] = short_left(x)[:, T:]

    def update(k, j, hi):
        terms = terms_ref[:, 3 * T * (k - before):3 * T * (k - before + 1)]
        d = dot_rows(terms, short_right(done_ref[k - before, (j - before) * T:(hi - before) * T, :]))
        for i in range(j, hi):
            put(i, get(i) - d[:, (i - j) * T:(i - j + 1) * T])

    work = []
    for k in range(before, first):
        work.append(lambda k=k: solve(k))
        for j in range(k + 1, NB, 2):
            work.append(lambda k=k, j=j: update(k, j, min(j + 2, NB)))
    return work


def fetch(source, target, sem):
    copy = pltpu.make_async_copy(source, target, sem)
    copy.start()
    return copy


def corner_part(first, last, refs):
    ids_ref = refs[0]
    others = []
    inputs = 4
    ins, refs = refs[1:1 + inputs], refs[1 + inputs:]
    count = 2 + (last < NB) + 3 * (first > 0)
    outs, refs = refs[:count], refs[count:]
    held, refs = refs[:count], refs[count:]
    done_ref, w_ref = held[:2]
    rest_ref = held[2] if last < NB else None
    s_ref, xl_ref, xr_ref, in_sems, out_sems = refs[:5]
    refs = refs[5:]
    sent = []

    def store(source, target):
        sent.append(fetch(source, target, out_sems.at[len(sent)]))

    def put(j, lo, hi, value):
        if j < last:
            done_ref[j - first, (lo - first) * T:(hi - first) * T, :] = value
        else:
            rest_ref[j - last, (lo - last) * T:(hi - last) * T, :] = value

    def get(j, lo, hi):
        if j < last:
            return done_ref[j - first, (lo - first) * T:(hi - first) * T, :]
        return rest_ref[j - last, (lo - last) * T:(hi - last) * T, :]

    rows = lax.broadcasted_iota(jnp.int32, (T, T), 0)
    lanes = lax.broadcasted_iota(jnp.int32, (T, T), 1)
    if first == 0:
        own_ref, other_ref, own_far_ref, other_far_ref = refs
        z = ids_ref[0]
        h = ids_ref[1]
        r = ids_ref[2]
        copies = [fetch(ins[n], refs[n], in_sems.at[n]) for n in range(inputs)]
        for copy in copies:
            copy.wait()

        def assemble(j, lo, hi):
            s = (z + NB - home(j)) % NB
            for i in range(lo, hi):
                t = (r + NB - i) % ROWS
                near = jnp.where(s > 4, s - 1, jnp.minimum(s, 3))
                value = jnp.where(
                    s == 4,
                    jnp.where(h == i // ROWS, own_far_ref[t], other_far_ref[t]),
                    jnp.where(h == i // ROWS, own_ref[near, t], other_ref[near, t]),
                )
                if i == j:
                    low = jnp.where(rows >= lanes, value, 0.0)
                    value = low + jnp.where(rows > lanes, value, 0.0).T
                put(j, i, i + 1, value)

        assemble(0, 0, 1)
        s_ref[...] = get(0, 0, 1)
        spare = [lambda: assemble(0, 1, NB)] + [lambda j=j: assemble(j, j, NB) for j in range(1, NB)]
    else:
        before = CUTS[CUTS.index(first) - 1]
        state_ref, old_ref, old_w_ref, x_ref, terms_ref, solved_ref, tile_ref, last_ref = refs
        parts_ref, column_ref, left_ref = held[-3:]
        width = first - before
        early = [
            fetch(ins[0].at[0, pl.ds(0, T)], tile_ref, in_sems.at[4]),
            fetch(ins[1].at[width - 1, pl.ds(width * T, (NB - first) * T)], last_ref, in_sems.at[5]),
        ]
        late = [fetch(ins[n], ref, in_sems.at[n]) for n, ref in enumerate((state_ref, old_ref, old_w_ref, x_ref))]
        for copy in early:
            copy.wait()
        xl_ref[first * T:(first + 1) * T, :] = left_terms(last_ref[:T, :], 1)
        xr_ref[first * T:(first + 1) * T, :] = right_terms(last_ref[:T, :], 1)
        s_ref[...] = tile_ref[...] - dot_rows(xl_ref[first * T:(first + 1) * T, :], xr_ref[first * T:(first + 1) * T, :])

        def take():
            late[0].wait()
            put(first, first + 1, NB, state_ref[0, T:, :])
            for j in range(first + 1, NB):
                put(j, j, NB, state_ref[j - first, (j - first) * T:, :])

        def last_terms():
            xl_ref[(first + 1) * T:, :] = left_terms(last_ref[T:, :], 1)
            xr_ref[(first + 1) * T:, :] = right_terms(last_ref[T:, :], 1)

        def arrive():
            for copy in late[1:]:
                copy.wait()

        spare = [take, last_terms, lambda: trail(first, first + 1)]
        for j in range(first + 1, NB, 2):
            spare.append((lambda j=j: trail_pair(j)) if j + 1 < NB else (lambda j=j: trail(j, j)))
        others = [arrive] + row_work(before, first, old_ref, old_w_ref, x_ref, parts_ref, left_ref, terms_ref, solved_ref)
    for j in range(first + 1, last):
        done_ref[j - first, :(j - first) * T, :] = jnp.zeros(((j - first) * T, T), jnp.float32)

    def panel(k, lo, hi):
        x = dot_rows(left_terms(get(k, lo, hi), 1), right_terms(w_ref[k - first], 1))
        put(k, lo, hi, x)
        xl_ref[lo * T:hi * T, :] = left_terms(x, 1)
        xr_ref[lo * T:hi * T, :] = right_terms(x, 1)

    def trail(j, lo):
        put(j, lo, NB, get(j, lo, NB) - dot_rows(xl_ref[lo * T:, :], xr_ref[j * T:(j + 1) * T, :]))

    def trail_pair(j):
        d = dot_rows(xl_ref[j * T:, :], xr_ref[j * T:(j + 2) * T, :])
        put(j, j, NB, get(j, j, NB) - d[:, :T])
        put(j + 1, j + 1, NB, get(j + 1, j + 1, NB) - d[T:, T:])

    for k in range(first, last):
        share = -(-len(others) // (last - k))
        spare, others = spare + others[:share], others[share:]
        factor_tile(s_ref, w_ref.at[k - first], spare)
        put(k, k, k + 1, s_ref[...].T)
        if k > first:
            store(done_ref.at[k - 1 - first], outs[0].at[k - 1 - first])
        n = k + 1
        if n == last:
            if first > 0:
                column_ref[...] = solved_ref[jnp.clip(ids_ref[3] - before, 0, first - before - 1)]
            for i in range(1, count):
                store(held[i], outs[i])
            if n < NB:
                panel(k, n, NB)
            break
        panel(k, n, n + 1)
        s_ref[...] = get(n, n, n + 1) - dot_rows(xl_ref[n * T:(n + 1) * T, :], xr_ref[n * T:(n + 1) * T, :])
        spare = []
        if n + 1 < NB:
            spare.append(lambda k=k, n=n: panel(k, n + 1, NB))
            spare.append(lambda n=n: trail(n, n + 1))
            for j in range(n + 1, NB, 2):
                if j + 1 < NB:
                    spare.append(lambda j=j: trail_pair(j))
                else:
                    spare.append(lambda j=j: trail(j, j))
    store(done_ref.at[last - 1 - first], outs[0].at[last - 1 - first])
    for copy in sent:
        copy.wait()


def corner_call(part, ids, *state):
    first, last = CUTS[part], CUTS[part + 1]
    smem = pl.BlockSpec(memory_space=pltpu.SMEM)
    far = pl.BlockSpec(memory_space=pl.ANY)
    span = (NB - first) * T
    shapes = [((last - first, span, T), jnp.float32), ((last - first, T, T), jnp.float32)]
    if last < NB:
        shapes.append(((NB - last, (NB - last) * T, T), jnp.float32))
    extra = [pltpu.VMEM(x.shape, x.dtype) for x in state]
    if first > 0:
        width = first - CUTS[part - 1]
        shapes.append(((6 * T, 2 * T * width), jnp.bfloat16))
        shapes.append(((6 * T, T), jnp.float32))
        shapes.append(((NB - first, 6 * T, T), jnp.float32))
        extra += [pltpu.VMEM((6 * T, 3 * T * width), jnp.bfloat16), pltpu.VMEM((width, 6 * T, T), jnp.float32)]
        extra += [pltpu.VMEM((T, T), jnp.float32), pltpu.VMEM((span, T), jnp.float32)]

    def kernel(*refs):
        corner_part(first, last, refs)

    return pl.pallas_call(
        kernel,
        in_specs=[smem] + [far] * len(state),
        out_specs=[far] * len(shapes),
        out_shape=[jax.ShapeDtypeStruct(*x) for x in shapes],
        scratch_shapes=[pltpu.VMEM(*x) for x in shapes]
        + [
            pltpu.VMEM((T, T), jnp.float32),
            pltpu.VMEM((NB * T, 6 * T), jnp.bfloat16),
            pltpu.VMEM((NB * T, 6 * T), jnp.bfloat16),
            pltpu.SemaphoreType.DMA((len(state) + 2,)),
            pltpu.SemaphoreType.DMA((last - first + len(shapes) - 1,)),
            *extra,
        ],
        compiler_params=params(),
    )(ids, *state)


def last_kernel(*refs):
    ids_ref, mark_ref = refs[:2]
    count = 3 * PARTS + 2
    ins, refs = refs[2:2 + count], refs[2 + count:]
    sent_in, refs = refs[:4], refs[4:]
    column_in, refs = refs[:PARTS - 1], refs[PARTS - 1:]
    out_ref = refs[0]
    held, refs = refs[1:1 + count], refs[1 + count:]
    done_refs, w_refs, parts_refs = held[:PARTS], held[PARTS:2 * PARTS], held[2 * PARTS:3 * PARTS - 1]
    left_ref, front_ref, tiles_ref = held[3 * PARTS - 1:]
    sent_ref, column_ref, x_ref, xa_ref, xb_ref, pad_ref, sems = refs
    behind = CUTS[-2]
    r = ids_ref[2]
    c = ids_ref[3]
    which = (r + ROWS - c % ROWS) % ROWS
    for s, ref in enumerate(sent_in):
        @pl.when(which == s)
        def _(ref=ref):
            fetch(ref, sent_ref, sems.at[count])

    copies = [None] * count
    order = [n for part in range(PARTS) for n in (part, PARTS + part)] + [3 * PARTS - 1]
    for n in order + [n for n in range(count) if n not in order]:
        copies[n] = fetch(ins[n], held[n], sems.at[n])
    pltpu.make_async_copy(sent_in[0], sent_ref, sems.at[count]).wait()
    for k in range(NB):
        x_ref[k, :2 * T] = sent_ref[home(k)].reshape(2 * T, T)

    rows = 8 * T
    for k in range(NB):
        part = sum(k >= cut for cut in CUTS[1:-1])
        first = CUTS[part]
        done_ref, w_ref = done_refs[part], w_refs[part]
        if k == first:
            copies[part].wait()
            copies[PARTS + part].wait()
        if k == behind:
            copies[3 * PARTS - 1].wait()
            for j in range(behind, NB):
                x_ref[j, 2 * T:] = left_ref[j - behind]
        high = rows if k >= behind else 2 * T
        x = dot_rows(short_left(x_ref[k, :high]), short_right(w_ref[k - first]))
        x_ref[k, :high] = x
        xb_ref[:, 3 * T * k:3 * T * (k + 1)] = short_right(x[:2 * T])
        terms = short_left(x)
        if k >= behind:
            xa_ref[:, 3 * T * (k - behind):3 * T * (k - behind + 1)] = terms[2 * T:]
        for j in range(k + 1, NB, 2):
            hi = min(j + 2, NB)
            d = dot_rows(terms, short_right(done_ref[k - first, (j - first) * T:(hi - first) * T, :]))
            for i in range(j, hi):
                x_ref[i, :high] = x_ref[i, :high] - d[:, (i - j) * T:(i - j + 1) * T]
    for copy in copies[2 * PARTS:3 * PARTS - 1] + copies[3 * PARTS:]:
        copy.wait()
    for b in range(2):
        pad_ref[b] = front_ref[b, 2:]

    def add_tile(s, carry):
        mark = mark_ref[s] - 1

        @pl.when(mark >= 0)
        def _():
            b = mark // 8
            a = mark % 8 - 2
            pad_ref[b, a] = pad_ref[b, a] + tiles_ref[s, :T, :]

        return carry

    lax.fori_loop(0, 2 * COLS, add_tile, 0)
    pieces = []
    for n, ref in enumerate(parts_refs):
        for k in range(CUTS[n + 1] - CUTS[n]):
            h = ref[:, 2 * T * k:2 * T * k + T]
            pieces += [h, ref[:, 2 * T * k:2 * T * (k + 1)]]
    product = dot_rows(jnp.concatenate(pieces + [xa_ref[...]], 1), xb_ref[...])
    limit = ids_ref[4]
    lower = lax.broadcasted_iota(jnp.int32, (T, T), 0)
    lanes = lax.broadcasted_iota(jnp.int32, (T, T), 1)

    def padded(b):
        j = (b * COLS + c) * T + lanes
        tiles = []
        for a in range(6):
            i = ((a + 2) * ROWS + r) * T + lower
            unit = jnp.where(i == j, 1.0, 0.0)
            tiles.append(jnp.where(jnp.logical_and(i < limit, j < limit), pad_ref[b, a], unit))
        return jnp.concatenate(tiles, 0)

    in_panel = c < NB
    zeros = jnp.zeros((2 * T, T), jnp.float32)
    out_ref[pl.Slice(0, 2 * T, 2), :] = zeros
    out_ref[pl.Slice(1, 2 * T, 2), :] = zeros
    out_ref[pl.Slice(4 * T + 1, 6 * T, 2), :] = padded(1) - product[:, T:]

    @pl.when(jnp.logical_not(in_panel))
    def _():
        out_ref[pl.Slice(4 * T, 6 * T, 2), :] = padded(0) - product[:, :T]

    for n, ref in enumerate(column_in):
        @pl.when(jnp.logical_and(c >= CUTS[n], c < CUTS[n + 1]))
        def _(n=n, ref=ref):
            copy = fetch(ref, column_ref, sems.at[count + 1])
            copy.wait()
            out_ref[pl.Slice(4 * T, 6 * T, 2), :] = column_ref[...]

    @pl.when(jnp.logical_and(c >= behind, c < NB))
    def _():
        out_ref[pl.Slice(4 * T, 6 * T, 2), :] = x_ref[jnp.clip(c, behind, NB - 1), 2 * T:]

    for a in range(2):
        i = r + ROWS * a
        for part, ref in enumerate(done_refs):
            first, last = CUTS[part], CUTS[part + 1]

            @pl.when(jnp.logical_and(jnp.logical_and(c >= first, c < last), i >= first))
            def _(ref=ref, first=first, last=last, a=a):
                at = pl.multiple_of(jnp.maximum(i - first, 0) * T, T)
                out_ref[pl.Slice(2 * a * T, T, 2), :] = ref[jnp.clip(c - first, 0, last - first - 1), pl.ds(at, T), :]


def last_call(ids, marks, parts, sent, front, tiles):
    smem = pl.BlockSpec(memory_space=pltpu.SMEM)
    vmem = pl.BlockSpec(memory_space=pltpu.VMEM)
    far = pl.BlockSpec(memory_space=pl.ANY)
    operands = [p[0] for p in parts] + [p[1] for p in parts]
    operands += [p[-3] for p in parts[1:]] + [parts[-1][-1], front, tiles]
    others = list(sent) + [p[-2] for p in parts[1:]]
    return pl.pallas_call(
        last_kernel,
        in_specs=[smem, smem] + [far] * (len(operands) + len(others)),
        out_specs=vmem,
        out_shape=jax.ShapeDtypeStruct((16 * T, T), jnp.float32),
        scratch_shapes=[pltpu.VMEM(x.shape, x.dtype) for x in operands]
        + [
            pltpu.VMEM((NB, 2, T, T), jnp.float32),
            pltpu.VMEM((6 * T, T), jnp.float32),
            pltpu.VMEM((NB, NB * T, T), jnp.float32),
            pltpu.VMEM((6 * T, 3 * T * (NB - CUTS[-2])), jnp.bfloat16),
            pltpu.VMEM((2 * T, 3 * T * NB), jnp.bfloat16),
            pltpu.VMEM((2, 6, T, T), jnp.float32),
            pltpu.SemaphoreType.DMA((len(operands) + 2,)),
        ],
        compiler_params=params(),
    )(ids, marks, *operands, *others)


def scatter_kernel(ids_ref, owner_ref, row_ref, col_ref, tiles_ref, keep_ref, give_ref, raw_ref):
    z = ids_ref[0]
    h = ids_ref[1]
    keep_ref[...] = jnp.zeros(keep_ref.shape, jnp.float32)
    give_ref[...] = jnp.zeros(give_ref.shape, jnp.float32)

    def step(i, carry):
        o = owner_ref[i]
        a = row_ref[i]
        b = col_ref[i]
        panel = jnp.logical_and(b == 0, o < NB)

        @pl.when(panel)
        def _():
            core = jnp.where(a < 2, a, (a - 2) // 3)
            place = jnp.where(a < 2, 0, a - 1 - 3 * core)
            p = (jnp.where(o % 2 == 0, o // 2, NB - 1 - o // 2) + NB - z) % NB

            @pl.when(core == h)
            def _():
                keep_ref[p, place] = keep_ref[p, place] + tiles_ref[i]

            @pl.when(core != h)
            def _():
                give_ref[p, place] = give_ref[p, place] + tiles_ref[i]

        mark = jnp.where(jnp.logical_or(panel, a < 2), 0, o * 16 + b * 8 + a + 1)
        raw_ref[i, :T, :] = tiles_ref[i]
        raw_ref[i, T:, :] = jnp.full((8, T), mark.astype(jnp.float32), jnp.float32)
        return carry

    lax.fori_loop(0, owner_ref.shape[0], step, 0)


def scatter_call(ids, owner, row, col, tiles):
    smem = pl.BlockSpec(memory_space=pltpu.SMEM)
    vmem = pl.BlockSpec(memory_space=pltpu.VMEM)
    return pl.pallas_call(
        scatter_kernel,
        in_specs=[smem, smem, smem, smem, vmem],
        out_specs=[vmem, vmem, vmem],
        out_shape=[
            jax.ShapeDtypeStruct((NB, 4, T, T), jnp.float32),
            jax.ShapeDtypeStruct((NB, 4, T, T), jnp.float32),
            jax.ShapeDtypeStruct((COLS, T + 8, T), jnp.float32),
        ],
        compiler_params=params(16 * 1024 * 1024),
    )(ids, owner, row, col, tiles)


def slot_kernel(mark_ref, raw_ref, send_ref, count_ref):
    for o in range(COLS):
        send_ref[2 * o, T:, :] = jnp.zeros((8, T), jnp.float32)
        send_ref[2 * o + 1, T:, :] = jnp.zeros((8, T), jnp.float32)
        count_ref[o] = 0

    def step(i, carry):
        mark = mark_ref[i] - 1

        @pl.when(mark >= 0)
        def _():
            o = mark // 16
            slot = 2 * o + count_ref[o]
            count_ref[o] = count_ref[o] + 1
            send_ref[slot, :T, :] = raw_ref[i, :T, :]
            send_ref[slot, T:, :] = jnp.full((8, T), (mark % 16 + 1).astype(jnp.float32), jnp.float32)

        return carry

    lax.fori_loop(0, COLS, step, 0)


def slot_call(marks, raw):
    smem = pl.BlockSpec(memory_space=pltpu.SMEM)
    vmem = pl.BlockSpec(memory_space=pltpu.VMEM)
    return pl.pallas_call(
        slot_kernel,
        in_specs=[smem, vmem],
        out_specs=vmem,
        out_shape=jax.ShapeDtypeStruct((2 * COLS, T + 8, T), jnp.float32),
        scratch_shapes=[pltpu.SMEM((COLS,), jnp.int32)],
        compiler_params=params(),
    )(marks, raw)


def moved(value, axes, pairs):
    return lax.ppermute(value, axes, pairs)


def together(*values):
    return lax.optimization_barrier(values)


def after(value, *others):
    return lax.optimization_barrier((value, *others))[0]


def on_device(front, child_tiles, child_owner, child_row, child_col, front_size):
    r = lax.axis_index("row")
    c = lax.axis_index("col")
    z = c // 2
    h = c % 2
    limit = front_size[0]
    stored = front.reshape(8, T, 2, T).transpose(2, 0, 1, 3)
    ids = jnp.stack([z, h, r, c, limit]).astype(jnp.int32)
    next_front = [(f, (f + 1) % 4) for f in range(4)]
    ahead_one = [(i, (i + 2) % COLS) for i in range(COLS)]
    behind_one = [(i, (i - 2) % COLS) for i in range(COLS)]
    swap = [(i, i ^ 1) for i in range(COLS)]
    both_axes = ("front", "col")
    hop = [(f * COLS + i, (f + 1) % 4 * COLS + i) for f in range(4) for i in range(COLS)]
    hop_ahead = [(f * COLS + i, (f + 1) % 4 * COLS + (i + 2) % COLS) for f in range(4) for i in range(COLS)]

    keep, give, raw = scatter_call(ids, child_owner[0, :, 0], child_row[0], child_col[0], child_tiles[0])

    to_even = [(j, 2 * home(j)) for j in range(NB)]
    to_odd = [(j, 2 * home(j) + 1) for j in range(NB)]
    corner_front = jnp.where(h == 0, moved(stored[0, :1], "col", to_even), moved(stored[0, 1:2], "col", to_odd))

    chunk = keep + moved(give, "col", swap)
    up = chunk[4]
    down = chunk[5]
    for s, t in ((3, 6), (2, 7), (1, 0)):
        up, down = together(moved(up, "col", ahead_one), moved(down, "col", behind_one))
        if s == 3:
            up, down, corner_front = together(up, down, corner_front)
        if s == 1:
            up, down, raw = together(up, down, moved(raw, "front", next_front))
        up = chunk[s] + up
        down = chunk[t] + down
    corner = corner_front + moved(down[:1], both_axes, hop) + moved(up[:1], both_axes, hop_ahead)

    quad = jnp.concatenate(
        [corner] + [moved(corner, "row", [(i, (i + s) % ROWS) for i in range(ROWS)]) for s in (1, 2, 3)], 0
    )

    body_front = after(stored[0, 2:], down)
    body_front = jnp.where(h == 0, moved(body_front[:3], "col", to_even), moved(body_front[3:], "col", to_odd))
    quad, body_front = together(quad, body_front)
    up, down = after([up, down], quad)
    body = body_front + moved(down[1:], both_axes, hop) + moved(up[1:], both_axes, hop_ahead)
    half_rows = ((2 + 3 * h + jnp.arange(3)) * ROWS + r)[:, None, None]
    body = jnp.where(half_rows * T + jnp.arange(T)[:, None] < limit, body, 0.0)
    gathered = lax.all_gather(body, "col", axis=0, tiled=False).reshape(NB, 6, T, T)

    pieces = {0: quad}
    ahead = behind = quad
    for s in (1, 2, 3):
        ahead, behind = together(moved(ahead, "col", ahead_one), moved(behind, "col", behind_one))
        pieces[s] = ahead
        pieces[NB - s] = behind
    own = jnp.stack([pieces[s] for s in sorted(pieces)])
    far, other = together(moved(behind, "col", behind_one), moved(own, "col", swap))
    other_far = moved(far, "col", swap)

    raw = after(raw, quad)
    send = slot_call(raw[:, T, 0].astype(jnp.int32), raw)
    arrived = lax.all_to_all(after(send, far), "col", split_axis=0, concat_axis=0, tiled=True)
    part0 = corner_call(0, after(ids, body), own, other, far, other_far)

    first_done = part0[1]

    gathered = after(gathered, first_done)
    pick = [jnp.maximum(c // ROWS - 2, 0), c // ROWS + 2]
    chosen = jnp.concatenate([lax.dynamic_slice_in_dim(gathered, p, 1, axis=1) for p in pick], 1)
    sent = [chosen]
    for s in (1, 2, 3):
        pairs = [(i % ROWS * COLS + i, (i % ROWS + s) % ROWS * COLS + i) for i in range(COLS)]
        sent.append(moved(chosen, ("row", "col"), pairs))
    parts = [part0, corner_call(1, after(ids, chosen), part0[2], part0[0], part0[1], gathered.reshape(NB, 6 * T, T))]
    arrived = after(arrived, parts[1][1])
    for part in range(2, PARTS):
        old = parts[-1]
        parts.append(corner_call(part, ids, old[2], old[0], old[1], old[-1]))
    marks = arrived[:, T, 0].astype(jnp.int32)
    result = last_call(ids, marks, parts, sent, stored, arrived)
    return result.reshape(front.shape)


def solution(mesh):
    spec = P("front", None, "row", None, None, "col", None)
    placed = (
        spec,
        P("front", ("row", "col"), None, None),
        P("front", ("row", "col"), None),
        P("front", ("row", "col")),
        P("front", ("row", "col")),
        P("front"),
    )
    return jax.shard_map(on_device, mesh=mesh, in_specs=placed, out_specs=spec, check_vma=False)
```
